32 devices in a mesh: ep: 16 (over z, x, core), dp: 2 (over y).
Axes of the slice: x: 2, y: 2, z: 4, core: 2. Of those that a mesh axis runs over, the one named last changes fastest.
Arguments:
- hidden: bfloat16 [4, 16, 256, 768], P('dp', 'ep'), parts along dimension 0, may hold values from -6 to 6
- down_weight: bfloat16 [16, 768, 2048], P('ep'), may hold values from -0.21875 to 0.21875
- routes: int32 [4, 256, 8], P('dp', 'ep'), parts along dimension 0, may hold values from 0 to 15, all different within a row; in each aligned block of 16 rows (0 to 15, 16 to 31, ..., all dimensions but the last counted through in order) at most 16 rows name the same one
- route_weight: float32 [4, 256, 8], P('dp', 'ep'), parts along dimension 0, may hold values from 0.03 to 0.4
- residual: bfloat16 [4, 256, 2048], P('dp', 'ep'), parts along dimension 0, may hold values from -6 to 6
Outputs:
- mixed: bfloat16 [4, 256, 2048], P('dp', 'ep'), parts along dimension 0
The draws below stay inside these ranges and needn't reach their ends.
There are 2 independent parts, one for each index of `dp`. The reference program is written for one: setup_inputs(seed, part) draws one part's arguments, and reference() takes and returns one part's arrays. A program takes and returns all parts, laid end to end along the dimension named above; an argument that names none is the same for every part. Nothing has to cross between parts.
Inputs may be any that keep to these rules, and one draw needn't show every extreme that they name: `routes`: each row names 8 different experts. In each micro-batch the 16 rows of one device name no expert more than 16 times, and in every draw some device's rows name some expert exactly 16 times.
All inputs are finite; a program needn't handle non-finite values.
Results may differ from the reference program's by a relative error of at most 0.0031.
Values may be sent and summed in bfloat16 or wider, within the bound.
A program may use at most 64 MiB of HBM per device.

```python
import math
import jax
import jax.numpy as jnp
import numpy as np
from jax import lax

D = 2048
H = 768
TOP = 8
BATCHES = 2
MB_TOK = 16
EXPERTS = 16
MOST = 16
SLOTS = 256
TOKENS = 256
N_EP = 16


def shard_levels(own_key, shape, split, smallest, top_value):
    loudness = 1.0
    for dim, shards_of in split:
        steps = jax.random.uniform(jax.random.fold_in(jax.random.fold_in(own_key, 6), dim), (shards_of,), jnp.float32, smallest / len(split), top_value / len(split))
        loudness = loudness * jnp.repeat(jnp.exp(steps), shape[dim] // shards_of).reshape((-1,) + (1,) * (len(shape) - 1 - dim))
    return loudness


def deal_out(key, own, number, rows, number_of, top, limit, slope):
    ranking = jax.random.permutation(key, number_of)
    heavy_load, common = portions_of(number_of, rows * top, limit, slope, True), portions_of(number_of, rows * top, limit, slope, False)
    places = jnp.arange(number_of)

    def named(lengths, rotation):
        used = int((lengths > 0).sum())
        fixed = max(1, used // 4)
        moved = fixed + (places - fixed + rotation * (used - fixed)) % max(1, number_of - fixed)
        return jnp.zeros((number_of,), jnp.int32).at[ranking[jnp.where(places < fixed, places, moved)]].set(jnp.asarray(lengths, jnp.int32))

    lengths = jnp.where(number % 4 == 0, named(heavy_load, number // 4), named(common, number - number // 4 - 1))
    mixed = jax.random.permutation(jax.random.fold_in(own, 3), number_of)
    source_of, sink = mixed[0:number_of // 2 * 2:2], mixed[1:number_of // 2 * 2:2]
    slack = jnp.minimum(lengths[source_of] - 1, limit - lengths[sink]) // 2
    slack = jnp.where((source_of == ranking[0]) | (sink == ranking[0]) | (lengths[sink] == 0), 0, jnp.maximum(slack, 0))
    moved = jax.random.randint(jax.random.fold_in(own, 4), (number_of // 2,), 0, 1 << 20) % (slack + 1)
    lengths = lengths.at[source_of].add(-moved).at[sink].add(moved)
    items = jnp.searchsorted(jnp.cumsum(lengths), jnp.arange(rows * top), side="right").astype(jnp.int32)
    listing = items.reshape(top, rows).T
    listing = listing[jax.random.permutation(jax.random.fold_in(own, 1), rows)]
    rotation = jax.random.randint(jax.random.fold_in(own, 2), (rows, 1), 0, top)
    return jnp.take_along_axis(listing, (jnp.arange(top)[None, :] + rotation) % top, axis=1)


def portions_of(number_of, total, reach, lean, full):
    portions = [(1 << 20) // math.isqrt(standing ** lean) + 1 for standing in range(1, number_of + 1)]
    largest = reach if full else min(reach, max(-(-total // number_of), total * portions[0] // sum(portions)))
    least = 1 if total - largest >= number_of - 1 else 0
    holding, rest = [largest] + [least] * (number_of - 1), total - largest - least * (number_of - 1)
    while rest > 0:
        movable = [i for i in range(1, number_of) if holding[i] < largest] or [i for i in range(1, number_of) if holding[i] < reach]
        pool, remaining = sum([portions[i] for i in movable]), rest
        for i in movable:
            extra = min(reach - holding[i], max(1, remaining * portions[i] // pool), rest)
            holding[i] = holding[i] + extra
            rest = rest - extra
    return np.array(holding)


def scatter_about(key, dims, spread, limit, cuts=(), held_as=jnp.bfloat16):
    result = jax.random.normal(key, dims, jnp.float32) * spread
    if len(cuts) > 0:
        result = shard_levels(key, dims, cuts, -0.22, 0.18) * result
    return jnp.clip(result, min=-limit, max=limit).astype(held_as)


def setup_inputs(seed: int = 0, part: int = 0) -> dict:
    streams_of = jax.random.split(jax.random.key(seed), 6)
    own_keys = jax.random.split(jax.random.fold_in(streams_of[5], part), 6)
    hidden = scatter_about(own_keys[0], (BATCHES, EXPERTS, SLOTS, H), 1.0, 6.0, ((1, 16),))
    down_weight = scatter_about(streams_of[1], (EXPERTS, H, D), H ** -0.5, 0.21875, ((0, 16),))
    routes_keys = jax.random.split(jax.random.fold_in(own_keys[2], 1), BATCHES * TOKENS // MB_TOK)
    routes_turns = jax.random.permutation(jax.random.fold_in(own_keys[2], 3), BATCHES * TOKENS // MB_TOK)
    routes = jax.vmap(lambda own, number: deal_out(jax.random.fold_in(own_keys[2], 2), own, number, MB_TOK, EXPERTS, TOP, MOST, 3))(routes_keys, routes_turns).reshape((BATCHES, TOKENS, TOP))
    route_weight = jnp.clip(jnp.exp(math.log(0.4) - 2.5902672 * jax.random.uniform(own_keys[3], (BATCHES, TOKENS, TOP), jnp.float32) ** shard_levels(own_keys[3], (BATCHES, TOKENS, TOP), ((1, 16),), -0.2, 0.2)), 0.03, 0.4)
    residual = scatter_about(own_keys[4], (BATCHES, TOKENS, D), 1.0, 6.0, ((1, 16),))
    return {"hidden": hidden, "down_weight": down_weight, "routes": routes, "route_weight": route_weight, "residual": residual}


def placement_of(routes_one):
    labels = jnp.arange(EXPERTS, dtype=jnp.int32)
    picked = jnp.sum((routes_one[:, :, None] == labels[None, None, :]).astype(jnp.int32), axis=1, dtype=jnp.int32)
    blocks = picked.reshape(N_EP, MB_TOK, EXPERTS)
    counts = jnp.sum(blocks, axis=1, dtype=jnp.int32)
    offsets = jnp.cumsum(counts, axis=0, dtype=jnp.int32) - counts
    before = jnp.cumsum(blocks, axis=1, dtype=jnp.int32) - blocks
    places = (offsets[:, None, :] + before).reshape(TOKENS, EXPERTS)
    position = jnp.take_along_axis(places, routes_one, axis=1).astype(jnp.int32)
    return position, jnp.sum(counts, axis=0, dtype=jnp.int32)


def one_batch(hidden_one, down_weight, routes_one, weight_one, residual_one):
    position, totals = placement_of(routes_one)
    token_ids = jnp.broadcast_to(jnp.arange(TOKENS, dtype=jnp.int32)[:, None], routes_one.shape)
    owners = jnp.zeros((EXPERTS, SLOTS), jnp.int32).at[routes_one, position].set(token_ids)
    shares = jnp.zeros((EXPERTS, SLOTS), jnp.float32).at[routes_one, position].set(weight_one)

    def visit_expert(summed, inputs):
        rows_in, matrix, owner_ids, share_row, live_rows = inputs

        def add_block(block_index, summed_in):
            begin_at = (block_index * 8).astype(jnp.int32)
            segment = lax.dynamic_slice_in_dim(rows_in, begin_at, 8, 0)
            product = jnp.dot(segment, matrix, preferred_element_type=jnp.float32).astype(jnp.bfloat16)
            product = lax.optimization_barrier(product).astype(jnp.float32)
            targets = lax.dynamic_slice_in_dim(owner_ids, begin_at, 8, 0)
            factor = lax.dynamic_slice_in_dim(share_row, begin_at, 8, 0)
            return summed_in.at[targets].add(factor[:, None] * product)

        block_count = ((live_rows + 7) // 8).astype(jnp.int32)
        return lax.fori_loop(jnp.int32(0), block_count, add_block, summed), None

    summed = jnp.zeros((TOKENS, D), jnp.float32)
    summed, _ = lax.scan(visit_expert, summed, (hidden_one, down_weight, owners, shares, totals))
    return (residual_one.astype(jnp.float32) + summed).astype(jnp.bfloat16)


def reference(hidden, down_weight, routes, route_weight, residual):
    results = [one_batch(hidden[batch_index], down_weight, routes[batch_index], route_weight[batch_index], residual[batch_index]) for batch_index in range(BATCHES)]
    return jnp.stack(results, axis=0)
```

```python
import functools
import math

import jax
import jax.numpy as jnp
from jax import lax
from jax.experimental import pallas as pl
from jax.experimental.pallas import tpu as pltpu
from jax.sharding import PartitionSpec as P


def shards(hidden, down_weight, routes, route_weight, residual):
    ranks_total = lax.axis_size("ep")
    batch_count = routes.shape[0]
    row_count = routes.shape[1]
    choose_count = routes.shape[2]
    slot_count = hidden.shape[2]
    per_peer = slot_count // ranks_total
    model_width = down_weight.shape[2]
    matrix = down_weight[0]
    labels = jnp.arange(ranks_total, dtype=jnp.int32)
    picked = jnp.sum((routes[:, :, :, None] == labels).astype(jnp.int32), axis=2, dtype=jnp.int32)
    rank_in_block = jnp.take_along_axis(
        jnp.cumsum(picked, axis=1, dtype=jnp.int32) - picked, routes, axis=2
    )
    loads_out = jnp.transpose(jnp.sum(picked, axis=1, dtype=jnp.int32))
    loads_in = lax.all_to_all(loads_out, "ep", split_axis=0, concat_axis=0, tiled=True)
    arriving = jnp.transpose(loads_in)
    offsets = jnp.cumsum(arriving, axis=1, dtype=jnp.int32) - arriving
    totals = jnp.sum(arriving, axis=1, dtype=jnp.int32)
    results = []
    for batch_index in range(batch_count):
        packed = hidden[batch_index, 0]
        block_size = math.gcd(slot_count, 128)

        def add_block(block_index, produced_in):
            begin_at = block_index * block_size
            segment = lax.dynamic_slice_in_dim(packed, begin_at, block_size, 0)
            product = jnp.dot(segment, matrix, preferred_element_type=jnp.float32).astype(
                jnp.bfloat16
            )
            return lax.dynamic_update_slice_in_dim(produced_in, product, begin_at, 0)

        block_count = (totals[batch_index] + block_size - 1) // block_size
        expert_produced = lax.fori_loop(
            0, block_count, add_block, jnp.zeros((slot_count, model_width), jnp.bfloat16)
        )
        selector = offsets[batch_index][:, None] + jnp.arange(per_peer, dtype=jnp.int32)[None, :]
        selector = jnp.minimum(selector, slot_count - 1)
        sending = jnp.take(expert_produced, selector.reshape(-1), axis=0).reshape(
            ranks_total, per_peer, model_width
        )
        arrived = lax.all_to_all(sending, "ep", split_axis=0, concat_axis=0, tiled=True)
        flattened = arrived.reshape(ranks_total * per_peer, model_width)
        location = routes[batch_index] * per_peer + rank_in_block[batch_index]
        gathered = jnp.take(flattened, location.reshape(-1), axis=0).reshape(
            row_count, choose_count, model_width
        )
        weighted = jnp.sum(
            route_weight[batch_index][:, :, None] * gathered.astype(jnp.float32), axis=1
        )
        results.append((residual[batch_index].astype(jnp.float32) + weighted).astype(jnp.bfloat16))
    return jnp.stack(results, axis=0)


MESH = pl.DeviceIdType.MESH
TILE = 512


def dense_kernel(
    sizes, hidden_hbm, weight_hbm, routes_hbm, shares_hbm, residual_hbm, mixed_ref,
    hidden, weight, routes, shares, residual, produced,
    note_out, note_in, slot_of,
    core_out, core_in, core_kept, x_out, x_in, x_kept, z_out, z_in,
    load_sem, column_sem, note_send, note_recv, core_send, core_recv, x_send, x_recv, z_send, z_recv,
):
    ranks, batches, rows, chosen, slots, width = sizes
    both = batches * rows
    me = lax.axis_index("ep")
    core, x, z = lax.rem(me, 2), lax.rem(me // 2, 2), me // 4
    low, high = lax.rem(z, 2), z // 2
    sibling = me + 1 - 2 * core
    beside = me + 2 - 4 * x
    near = me + 4 - 8 * low
    far = me + 8 - 16 * high

    barrier = pltpu.get_barrier_semaphore()

    def greet(step, carry):
        pl.semaphore_signal(
            barrier, inc=1, device_id={"ep": lax.rem(me + step, ranks)}, device_id_type=MESH
        )
        return carry

    lax.fori_loop(1, ranks, greet, 0)

    loads = [
        pltpu.make_async_copy(routes_hbm, routes, load_sem.at[0]),
        pltpu.make_async_copy(shares_hbm, shares, load_sem.at[1]),
        pltpu.make_async_copy(hidden_hbm, hidden, load_sem.at[2]),
    ]
    columns = [
        pltpu.make_async_copy(
            weight_hbm.at[:, pl.ds(j * TILE, TILE)], weight.at[j], column_sem.at[j]
        )
        for j in range(width // TILE)
    ]
    residual_load = pltpu.make_async_copy(residual_hbm, residual, load_sem.at[3])
    for copy in loads + columns + [residual_load]:
        copy.start()

    loads[0].wait()
    loads[1].wait()
    expert = lax.broadcasted_iota(jnp.int32, (both, 128), 1)
    given = jnp.zeros((both, 128), jnp.float32)
    named = jnp.zeros((both, 128), jnp.float32)
    route_rows, share_rows = routes[...], shares[...]
    for k in range(chosen):
        hit = route_rows[:, k : k + 1] == expert
        given = given + jnp.where(hit, share_rows[:, k : k + 1], 0.0)
        named = named + jnp.where(hit, 1.0, 0.0)
    notes = jnp.concatenate(
        [given, named, jnp.zeros((128 - 2 * both, 128), jnp.float32)], axis=0
    )
    notes = jnp.transpose(notes)[:ranks]
    note_out[...] = notes.reshape(ranks, 1, 128)
    note_in[pl.ds(me, 1)] = note_out[pl.ds(me, 1)]

    pl.semaphore_wait(barrier, ranks - 1)

    def note_to(step):
        peer = lax.rem(me + step, ranks)
        return pltpu.make_async_remote_copy(
            src_ref=note_out.at[peer],
            dst_ref=note_in.at[me],
            send_sem=note_send.at[peer],
            recv_sem=note_recv.at[me],
            device_id={"ep": peer},
            device_id_type=MESH,
        )

    def note_from(step):
        peer = lax.rem(me + step, ranks)
        return pltpu.make_async_remote_copy(
            src_ref=note_out.at[peer],
            dst_ref=note_in.at[peer],
            send_sem=note_send.at[peer],
            recv_sem=note_recv.at[peer],
            device_id={"ep": peer},
            device_id_type=MESH,
        )

    def send_note(step, carry):
        note_to(step).start()
        return carry

    lax.fori_loop(1, ranks, send_note, 0)

    loads[2].wait()
    for j in range(width // TILE):
        columns[j].wait()
        for b in range(batches):
            produced[b, :, j * TILE : (j + 1) * TILE] = jnp.dot(
                hidden[b], weight[j], preferred_element_type=jnp.float32
            ).astype(jnp.bfloat16)

    def take_note(step, carry):
        note_from(step).wait_recv()
        return carry

    lax.fori_loop(1, ranks, take_note, 0)

    flags = note_in[...].reshape(ranks, 128)
    upper = lax.broadcasted_iota(jnp.int32, (128, 128), 0)
    lower = lax.broadcasted_iota(jnp.int32, (128, 128), 1)
    alike = (upper >= both) & (upper < 2 * both) & (lower >= both) & (lower < 2 * both)
    alike = alike & (upper // rows == lower // rows)
    ones = jnp.where(alike, 1.0, 0.0).astype(jnp.bfloat16)
    ahead = jnp.where(alike & (upper < lower), 1.0, 0.0).astype(jnp.bfloat16)
    packed = flags.astype(jnp.bfloat16)
    within = jnp.dot(packed, ahead, preferred_element_type=jnp.float32)
    counts = jnp.dot(packed, ones, preferred_element_type=jnp.float32).astype(jnp.bfloat16)
    earlier = lax.broadcasted_iota(jnp.int32, (ranks, ranks), 1) < lax.broadcasted_iota(
        jnp.int32, (ranks, ranks), 0
    )
    before = jnp.dot(
        jnp.where(earlier, 1.0, 0.0).astype(jnp.bfloat16), counts, preferred_element_type=jnp.float32
    )
    slot_of[...] = jnp.where(flags > 0.5, within + before, -1.0).reshape(ranks, 1, 128)

    lane = lax.broadcasted_iota(jnp.int32, (both, 128), 1)
    row = lax.broadcasted_iota(jnp.int32, (both, 128), 0)
    slot = lax.broadcasted_iota(jnp.int32, (4 * rows, slots), 1).astype(jnp.float32)

    def core_copy(i):
        return pltpu.make_async_remote_copy(
            src_ref=core_out.at[i], dst_ref=core_in.at[i],
            send_sem=core_send.at[i], recv_sem=core_recv.at[i],
            device_id={"ep": sibling}, device_id_type=MESH,
        )

    def x_copy(i):
        return pltpu.make_async_remote_copy(
            src_ref=x_out.at[i], dst_ref=x_in.at[i],
            send_sem=x_send.at[i], recv_sem=x_recv.at[i],
            device_id={"ep": beside}, device_id_type=MESH,
        )

    def z_copy(i):
        return pltpu.make_async_remote_copy(
            src_ref=z_out.at[i], dst_ref=z_in.at[i],
            send_sem=z_send.at[i], recv_sem=z_recv.at[i],
            device_id={"ep": far if i == 1 else near}, device_id_type=MESH,
        )

    def spread(i):
        plane = 2 * lax.rem(high + 1 - i // 2, 2) + lax.rem(low + 1 - i % 2, 2)
        factor, place = [], []
        for other_core in (1, 0):
            for other_x in (1, 0):
                c = lax.rem(core + other_core, 2)
                at_x = lax.rem(x + other_x, 2)
                owner = plane * 4 + at_x * 2 + c
                factor.append(
                    jnp.sum(jnp.where(lane == row, note_in[owner], 0.0), axis=1, keepdims=True)
                )
                place.append(
                    jnp.sum(jnp.where(lane == row + both, slot_of[owner], 0.0), axis=1, keepdims=True)
                )
        for b in range(batches):
            span = slice(b * rows, (b + 1) * rows)
            scale = jnp.concatenate([f[span] for f in factor], axis=0)
            spot = jnp.concatenate([p[span] for p in place], axis=0)
            pick = jnp.where(spot == slot, 1.0, 0.0).astype(jnp.bfloat16)
            for j in range(width // TILE):
                cut = slice(j * TILE, (j + 1) * TILE)
                part = scale * jnp.dot(
                    pick, produced[b, :, cut], preferred_element_type=jnp.float32
                )
                core_out[i, b, :, cut] = part[: 2 * rows].astype(jnp.bfloat16)
                core_kept[i, b, :, cut] = part[2 * rows :]
        core_copy(i).start()

    def over_cores(i):
        core_copy(i).wait_recv()
        for b in range(batches):
            total = core_kept[i, b] + core_in[i, b].astype(jnp.float32)
            x_out[i, b] = total[:rows].astype(jnp.bfloat16)
            x_kept[i, b] = total[rows:]
        x_copy(i).start()

    def over_x(i):
        x_copy(i).wait_recv()
        return x_kept[i] + x_in[i].astype(jnp.float32)

    for i in range(4):
        spread(i)
        if i > 0:
            over_cores(i - 1)
    over_cores(3)

    z_out[0] = over_x(0).astype(jnp.bfloat16)
    z_copy(0).start()
    total = over_x(1)
    z_copy(0).wait_recv()
    z_out[1] = (total + z_in[0].astype(jnp.float32)).astype(jnp.bfloat16)
    z_copy(1).start()
    z_out[2] = over_x(2).astype(jnp.bfloat16)
    z_copy(2).start()
    residual_load.wait()
    total = over_x(3) + residual[...].astype(jnp.float32)
    z_copy(1).wait_recv()
    total = total + z_in[1].astype(jnp.float32)
    z_copy(2).wait_recv()
    mixed_ref[...] = (total + z_in[2].astype(jnp.float32)).astype(jnp.bfloat16)

    for i in range(4):
        core_copy(i).wait_send()
        x_copy(i).wait_send()
    for i in range(3):
        z_copy(i).wait_send()

    def note_left(step, carry):
        note_to(step).wait_send()
        return carry

    lax.fori_loop(1, ranks, note_left, 0)


def dense_shards(ranks, hidden, down_weight, routes, route_weight, residual):
    batches, rows, chosen = routes.shape
    slots, depth = hidden.shape[2:]
    width = down_weight.shape[2]
    both = batches * rows
    bf16, f32 = jnp.bfloat16, jnp.float32
    sizes = (ranks, batches, rows, chosen, slots, width)
    parts = 4
    return pl.pallas_call(
        functools.partial(dense_kernel, sizes),
        out_shape=jax.ShapeDtypeStruct((batches, rows, width), bf16),
        in_specs=[pl.BlockSpec(memory_space=pl.ANY)] * 5,
        out_specs=pl.BlockSpec(memory_space=pltpu.VMEM),
        scratch_shapes=[
            pltpu.VMEM((batches, slots, depth), bf16),
            pltpu.VMEM((width // TILE, depth, TILE), bf16),
            pltpu.VMEM((both, chosen), jnp.int32),
            pltpu.VMEM((both, chosen), f32),
            pltpu.VMEM((batches, rows, width), bf16),
            pltpu.VMEM((batches, slots, width), bf16),
            pltpu.VMEM((ranks, 1, 128), f32),
            pltpu.VMEM((ranks, 1, 128), f32),
            pltpu.VMEM((ranks, 1, 128), f32),
            pltpu.VMEM((parts, batches, 2 * rows, width), bf16),
            pltpu.VMEM((parts, batches, 2 * rows, width), bf16),
            pltpu.VMEM((parts, batches, 2 * rows, width), f32),
            pltpu.VMEM((parts, batches, rows, width), bf16),
            pltpu.VMEM((parts, batches, rows, width), bf16),
            pltpu.VMEM((parts, batches, rows, width), f32),
            pltpu.VMEM((3, batches, rows, width), bf16),
            pltpu.VMEM((3, batches, rows, width), bf16),
            pltpu.SemaphoreType.DMA((4,)),
            pltpu.SemaphoreType.DMA((width // TILE,)),
            pltpu.SemaphoreType.DMA((ranks,)),
            pltpu.SemaphoreType.DMA((ranks,)),
            pltpu.SemaphoreType.DMA((parts,)),
            pltpu.SemaphoreType.DMA((parts,)),
            pltpu.SemaphoreType.DMA((parts,)),
            pltpu.SemaphoreType.DMA((parts,)),
            pltpu.SemaphoreType.DMA((3,)),
            pltpu.SemaphoreType.DMA((3,)),
        ],
        compiler_params=pltpu.CompilerParams(
            collective_id=0, has_side_effects=True, vmem_limit_bytes=48 * 1024 * 1024
        ),
    )(
        hidden.reshape(batches, slots, depth),
        down_weight.reshape(depth, width),
        routes.reshape(both, chosen),
        route_weight.reshape(both, chosen),
        residual,
    )


def solution(mesh):
    ranks = mesh.shape["ep"]
    in_specs = (
        P("dp", "ep", None, None),
        P("ep", None, None),
        P("dp", "ep", None),
        P("dp", "ep", None),
        P("dp", "ep", None),
    )
    out_specs = P("dp", "ep", None)

    def run(hidden, down_weight, routes, route_weight, residual):
        rows = routes.shape[1] // ranks
        batches = routes.shape[0] // mesh.shape["dp"]
        dense = ranks == 16 and rows % 16 == 0 and routes.shape[1] <= hidden.shape[2]
        dense = dense and 2 * batches * rows <= 128
        body = functools.partial(dense_shards, ranks) if dense else shards
        return jax.shard_map(
            body, mesh=mesh, in_specs=in_specs, out_specs=out_specs, check_vma=False
        )(hidden, down_weight, routes, route_weight, residual)

    return run
```

```python
import functools
import math

import jax
import jax.numpy as jnp
from jax import lax
from jax.experimental import pallas as pl
from jax.experimental.pallas import tpu as pltpu
from jax.sharding import PartitionSpec as P


def shards(hidden, down_weight, routes, route_weight, residual):
    ranks_total = lax.axis_size("ep")
    batch_count = routes.shape[0]
    row_count = routes.shape[1]
    choose_count = routes.shape[2]
    slot_count = hidden.shape[2]
    per_peer = slot_count // ranks_total
    model_width = down_weight.shape[2]
    matrix = down_weight[0]
    labels = jnp.arange(ranks_total, dtype=jnp.int32)
    picked = jnp.sum((routes[:, :, :, None] == labels).astype(jnp.int32), axis=2, dtype=jnp.int32)
    rank_in_block = jnp.take_along_axis(
        jnp.cumsum(picked, axis=1, dtype=jnp.int32) - picked, routes, axis=2
    )
    loads_out = jnp.transpose(jnp.sum(picked, axis=1, dtype=jnp.int32))
    loads_in = lax.all_to_all(loads_out, "ep", split_axis=0, concat_axis=0, tiled=True)
    arriving = jnp.transpose(loads_in)
    offsets = jnp.cumsum(arriving, axis=1, dtype=jnp.int32) - arriving
    totals = jnp.sum(arriving, axis=1, dtype=jnp.int32)
    results = []
    for batch_index in range(batch_count):
        packed = hidden[batch_index, 0]
        block_size = math.gcd(slot_count, 128)

        def add_block(block_index, produced_in):
            begin_at = block_index * block_size
            segment = lax.dynamic_slice_in_dim(packed, begin_at, block_size, 0)
            product = jnp.dot(segment, matrix, preferred_element_type=jnp.float32).astype(
                jnp.bfloat16
            )
            return lax.dynamic_update_slice_in_dim(produced_in, product, begin_at, 0)

        block_count = (totals[batch_index] + block_size - 1) // block_size
        expert_produced = lax.fori_loop(
            0, block_count, add_block, jnp.zeros((slot_count, model_width), jnp.bfloat16)
        )
        selector = offsets[batch_index][:, None] + jnp.arange(per_peer, dtype=jnp.int32)[None, :]
        selector = jnp.minimum(selector, slot_count - 1)
        sending = jnp.take(expert_produced, selector.reshape(-1), axis=0).reshape(
            ranks_total, per_peer, model_width
        )
        arrived = lax.all_to_all(sending, "ep", split_axis=0, concat_axis=0, tiled=True)
        flattened = arrived.reshape(ranks_total * per_peer, model_width)
        location = routes[batch_index] * per_peer + rank_in_block[batch_index]
        gathered = jnp.take(flattened, location.reshape(-1), axis=0).reshape(
            row_count, choose_count, model_width
        )
        weighted = jnp.sum(
            route_weight[batch_index][:, :, None] * gathered.astype(jnp.float32), axis=1
        )
        results.append((residual[batch_index].astype(jnp.float32) + weighted).astype(jnp.bfloat16))
    return jnp.stack(results, axis=0)


MESH = pl.DeviceIdType.MESH
TILE = 512


def dense_kernel(
    sizes, hidden_hbm, weight_hbm, routes_hbm, shares_hbm, residual_hbm, mixed_ref,
    hidden, weight, routes, shares, residual, produced,
    note_out, note_in, slot_of,
    core_out, core_in, core_kept, x_out, x_in, x_kept, z_out, z_in,
    load_sem, column_sem, note_send, note_recv, core_send, core_recv, x_send, x_recv, z_send, z_recv,
):
    ranks, batches, rows, chosen, slots, width = sizes
    both = batches * rows
    me = lax.axis_index("ep")
    core, x, z = lax.rem(me, 2), lax.rem(me // 2, 2), me // 4
    low, high = lax.rem(z, 2), z // 2
    sibling = me + 1 - 2 * core
    beside = me + 2 - 4 * x
    near = me + 4 - 8 * low
    far = me + 8 - 16 * high

    barrier = pltpu.get_barrier_semaphore()

    def greet(step, carry):
        pl.semaphore_signal(
            barrier, inc=1, device_id={"ep": lax.rem(me + step, ranks)}, device_id_type=MESH
        )
        return carry

    lax.fori_loop(1, ranks, greet, 0)

    loads = [
        pltpu.make_async_copy(routes_hbm, routes, load_sem.at[0]),
        pltpu.make_async_copy(shares_hbm, shares, load_sem.at[1]),
        pltpu.make_async_copy(hidden_hbm, hidden, load_sem.at[2]),
    ]
    columns = [
        pltpu.make_async_copy(
            weight_hbm.at[:, pl.ds(j * TILE, TILE)], weight.at[j], column_sem.at[j]
        )
        for j in range(width // TILE)
    ]
    residual_load = pltpu.make_async_copy(residual_hbm, residual, load_sem.at[3])
    for copy in loads + columns + [residual_load]:
        copy.start()

    loads[0].wait()
    loads[1].wait()
    given, named = [], []
    expert = lax.broadcasted_iota(jnp.int32, (ranks, chosen, rows), 0)
    for b in range(batches):
        hit = routes[b][None] == expert
        given.append(jnp.sum(jnp.where(hit, shares[b][None], 0.0), axis=1))
        named.append(jnp.sum(jnp.where(hit, 1.0, 0.0), axis=1))
    notes = jnp.concatenate(
        given + named + [jnp.zeros((ranks, 128 - 2 * both), jnp.float32)], axis=1
    )
    note_out[...] = notes.reshape(ranks, 1, 128)
    note_in[pl.ds(me, 1)] = note_out[pl.ds(me, 1)]

    pl.semaphore_wait(barrier, ranks - 1)

    def note_to(step):
        peer = lax.rem(me + step, ranks)
        return pltpu.make_async_remote_copy(
            src_ref=note_out.at[peer],
            dst_ref=note_in.at[me],
            send_sem=note_send.at[peer],
            recv_sem=note_recv.at[me],
            device_id={"ep": peer},
            device_id_type=MESH,
        )

    def note_from(step):
        peer = lax.rem(me + step, ranks)
        return pltpu.make_async_remote_copy(
            src_ref=note_out.at[peer],
            dst_ref=note_in.at[peer],
            send_sem=note_send.at[peer],
            recv_sem=note_recv.at[peer],
            device_id={"ep": peer},
            device_id_type=MESH,
        )

    def send_note(step, carry):
        note_to(step).start()
        return carry

    lax.fori_loop(1, ranks, send_note, 0)

    loads[2].wait()
    for j in range(width // TILE):
        columns[j].wait()
        for b in range(batches):
            produced[b, :, j * TILE : (j + 1) * TILE] = jnp.dot(
                hidden[b], weight[j], preferred_element_type=jnp.float32
            ).astype(jnp.bfloat16)

    def take_note(step, carry):
        note_from(step).wait_recv()
        return carry

    lax.fori_loop(1, ranks, take_note, 0)

    flags = note_in[...].reshape(ranks, 128)
    upper = lax.broadcasted_iota(jnp.int32, (128, 128), 0)
    lower = lax.broadcasted_iota(jnp.int32, (128, 128), 1)
    alike = (upper >= both) & (upper < 2 * both) & (lower >= both) & (lower < 2 * both)
    alike = alike & (upper // rows == lower // rows)
    ones = jnp.where(alike, 1.0, 0.0).astype(jnp.bfloat16)
    ahead = jnp.where(alike & (upper < lower), 1.0, 0.0).astype(jnp.bfloat16)
    packed = flags.astype(jnp.bfloat16)
    within = jnp.dot(packed, ahead, preferred_element_type=jnp.float32)
    counts = jnp.dot(packed, ones, preferred_element_type=jnp.float32).astype(jnp.bfloat16)
    earlier = lax.broadcasted_iota(jnp.int32, (ranks, ranks), 1) < lax.broadcasted_iota(
        jnp.int32, (ranks, ranks), 0
    )
    before = jnp.dot(
        jnp.where(earlier, 1.0, 0.0).astype(jnp.bfloat16), counts, preferred_element_type=jnp.float32
    )
    slot_of[...] = jnp.where(flags > 0.5, within + before, -1.0).reshape(ranks, 1, 128)

    lane = lax.broadcasted_iota(jnp.int32, (both, 128), 1)
    row = lax.broadcasted_iota(jnp.int32, (both, 128), 0)
    slot = lax.broadcasted_iota(jnp.int32, (4 * rows, slots), 1).astype(jnp.float32)

    def core_copy(i):
        return pltpu.make_async_remote_copy(
            src_ref=core_out.at[i], dst_ref=core_in.at[i],
            send_sem=core_send.at[i], recv_sem=core_recv.at[i],
            device_id={"ep": sibling}, device_id_type=MESH,
        )

    def x_copy(i):
        return pltpu.make_async_remote_copy(
            src_ref=x_out.at[i], dst_ref=x_in.at[i],
            send_sem=x_send.at[i], recv_sem=x_recv.at[i],
            device_id={"ep": beside}, device_id_type=MESH,
        )

    def z_copy(i):
        return pltpu.make_async_remote_copy(
            src_ref=z_out.at[i], dst_ref=z_in.at[i],
            send_sem=z_send.at[i], recv_sem=z_recv.at[i],
            device_id={"ep": far if i == 1 else near}, device_id_type=MESH,
        )

    def spread(i):
        plane = 2 * lax.rem(high + 1 - i // 2, 2) + lax.rem(low + 1 - i % 2, 2)
        factor, place = [], []
        for other_core in (1, 0):
            for other_x in (1, 0):
                c = lax.rem(core + other_core, 2)
                at_x = lax.rem(x + other_x, 2)
                owner = plane * 4 + at_x * 2 + c
                factor.append(
                    jnp.sum(jnp.where(lane == row, note_in[owner], 0.0), axis=1, keepdims=True)
                )
                place.append(
                    jnp.sum(jnp.where(lane == row + both, slot_of[owner], 0.0), axis=1, keepdims=True)
                )
        for b in range(batches):
            span = slice(b * rows, (b + 1) * rows)
            scale = jnp.concatenate([f[span] for f in factor], axis=0)
            spot = jnp.concatenate([p[span] for p in place], axis=0)
            pick = jnp.where(spot == slot, 1.0, 0.0).astype(jnp.bfloat16)
            for j in range(width // TILE):
                cut = slice(j * TILE, (j + 1) * TILE)
                part = scale * jnp.dot(
                    pick, produced[b, :, cut], preferred_element_type=jnp.float32
                )
                core_out[i, b, :, cut] = part[: 2 * rows].astype(jnp.bfloat16)
                core_kept[i, b, :, cut] = part[2 * rows :]
        core_copy(i).start()

    def over_cores(i):
        core_copy(i).wait_recv()
        for b in range(batches):
            total = core_kept[i, b] + core_in[i, b].astype(jnp.float32)
            x_out[i, b] = total[:rows].astype(jnp.bfloat16)
            x_kept[i, b] = total[rows:]
        x_copy(i).start()

    def over_x(i):
        x_copy(i).wait_recv()
        return x_kept[i] + x_in[i].astype(jnp.float32)

    for i in range(4):
        spread(i)
        if i > 0:
            over_cores(i - 1)
    over_cores(3)

    z_out[0] = over_x(0).astype(jnp.bfloat16)
    z_copy(0).start()
    total = over_x(1)
    z_copy(0).wait_recv()
    z_out[1] = (total + z_in[0].astype(jnp.float32)).astype(jnp.bfloat16)
    z_copy(1).start()
    z_out[2] = over_x(2).astype(jnp.bfloat16)
    z_copy(2).start()
    residual_load.wait()
    total = over_x(3) + residual[...].astype(jnp.float32)
    z_copy(1).wait_recv()
    total = total + z_in[1].astype(jnp.float32)
    z_copy(2).wait_recv()
    mixed_ref[...] = (total + z_in[2].astype(jnp.float32)).astype(jnp.bfloat16)

    for i in range(4):
        core_copy(i).wait_send()
        x_copy(i).wait_send()
    for i in range(3):
        z_copy(i).wait_send()

    def note_left(step, carry):
        note_to(step).wait_send()
        return carry

    lax.fori_loop(1, ranks, note_left, 0)


def dense_shards(ranks, hidden, down_weight, routes, route_weight, residual):
    batches, rows, chosen = routes.shape
    slots, depth = hidden.shape[2:]
    width = down_weight.shape[2]
    both = batches * rows
    bf16, f32 = jnp.bfloat16, jnp.float32
    sizes = (ranks, batches, rows, chosen, slots, width)
    parts = 4
    return pl.pallas_call(
        functools.partial(dense_kernel, sizes),
        out_shape=jax.ShapeDtypeStruct((batches, rows, width), bf16),
        in_specs=[pl.BlockSpec(memory_space=pl.ANY)] * 5,
        out_specs=pl.BlockSpec(memory_space=pltpu.VMEM),
        scratch_shapes=[
            pltpu.VMEM((batches, slots, depth), bf16),
            pltpu.VMEM((width // TILE, depth, TILE), bf16),
            pltpu.VMEM((batches, chosen, rows), jnp.int32),
            pltpu.VMEM((batches, chosen, rows), f32),
            pltpu.VMEM((batches, rows, width), bf16),
            pltpu.VMEM((batches, slots, width), bf16),
            pltpu.VMEM((ranks, 1, 128), f32),
            pltpu.VMEM((ranks, 1, 128), f32),
            pltpu.VMEM((ranks, 1, 128), f32),
            pltpu.VMEM((parts, batches, 2 * rows, width), bf16),
            pltpu.VMEM((parts, batches, 2 * rows, width), bf16),
            pltpu.VMEM((parts, batches, 2 * rows, width), f32),
            pltpu.VMEM((parts, batches, rows, width), bf16),
            pltpu.VMEM((parts, batches, rows, width), bf16),
            pltpu.VMEM((parts, batches, rows, width), f32),
            pltpu.VMEM((3, batches, rows, width), bf16),
            pltpu.VMEM((3, batches, rows, width), bf16),
            pltpu.SemaphoreType.DMA((4,)),
            pltpu.SemaphoreType.DMA((width // TILE,)),
            pltpu.SemaphoreType.DMA((ranks,)),
            pltpu.SemaphoreType.DMA((ranks,)),
            pltpu.SemaphoreType.DMA((parts,)),
            pltpu.SemaphoreType.DMA((parts,)),
            pltpu.SemaphoreType.DMA((parts,)),
            pltpu.SemaphoreType.DMA((parts,)),
            pltpu.SemaphoreType.DMA((3,)),
            pltpu.SemaphoreType.DMA((3,)),
        ],
        compiler_params=pltpu.CompilerParams(
            collective_id=0, has_side_effects=True, vmem_limit_bytes=64 * 1024 * 1024
        ),
    )(
        hidden.reshape(batches, slots, depth),
        down_weight.reshape(depth, width),
        jnp.swapaxes(routes, 1, 2),
        jnp.swapaxes(route_weight, 1, 2),
        residual,
    )


def solution(mesh):
    ranks = mesh.shape["ep"]
    in_specs = (
        P("dp", "ep", None, None),
        P("ep", None, None),
        P("dp", "ep", None),
        P("dp", "ep", None),
        P("dp", "ep", None),
    )
    out_specs = P("dp", "ep", None)

    def run(hidden, down_weight, routes, route_weight, residual):
        rows = routes.shape[1] // ranks
        batches = routes.shape[0] // mesh.shape["dp"]
        dense = ranks == 16 and rows % 16 == 0 and routes.shape[1] <= hidden.shape[2]
        dense = dense and 2 * batches * rows <= 128
        body = functools.partial(dense_shards, ranks) if dense else shards
        return jax.shard_map(
            body, mesh=mesh, in_specs=in_specs, out_specs=out_specs, check_vma=False
        )(hidden, down_weight, routes, route_weight, residual)

    return run
```

```python
import functools
import math

import jax
import jax.numpy as jnp
from jax import lax
from jax.experimental import pallas as pl
from jax.experimental.pallas import tpu as pltpu
from jax.sharding import PartitionSpec as P


def shards(hidden, down_weight, routes, route_weight, residual):
    ranks_total = lax.axis_size("ep")
    batch_count = routes.shape[0]
    row_count = routes.shape[1]
    choose_count = routes.shape[2]
    slot_count = hidden.shape[2]
    per_peer = slot_count // ranks_total
    model_width = down_weight.shape[2]
    matrix = down_weight[0]
    labels = jnp.arange(ranks_total, dtype=jnp.int32)
    picked = jnp.sum((routes[:, :, :, None] == labels).astype(jnp.int32), axis=2, dtype=jnp.int32)
    rank_in_block = jnp.take_along_axis(
        jnp.cumsum(picked, axis=1, dtype=jnp.int32) - picked, routes, axis=2
    )
    loads_out = jnp.transpose(jnp.sum(picked, axis=1, dtype=jnp.int32))
    loads_in = lax.all_to_all(loads_out, "ep", split_axis=0, concat_axis=0, tiled=True)
    arriving = jnp.transpose(loads_in)
    offsets = jnp.cumsum(arriving, axis=1, dtype=jnp.int32) - arriving
    totals = jnp.sum(arriving, axis=1, dtype=jnp.int32)
    results = []
    for batch_index in range(batch_count):
        packed = hidden[batch_index, 0]
        block_size = math.gcd(slot_count, 128)

        def add_block(block_index, produced_in):
            begin_at = block_index * block_size
            segment = lax.dynamic_slice_in_dim(packed, begin_at, block_size, 0)
            product = jnp.dot(segment, matrix, preferred_element_type=jnp.float32).astype(
                jnp.bfloat16
            )
            return lax.dynamic_update_slice_in_dim(produced_in, product, begin_at, 0)

        block_count = (totals[batch_index] + block_size - 1) // block_size
        expert_produced = lax.fori_loop(
            0, block_count, add_block, jnp.zeros((slot_count, model_width), jnp.bfloat16)
        )
        selector = offsets[batch_index][:, None] + jnp.arange(per_peer, dtype=jnp.int32)[None, :]
        selector = jnp.minimum(selector, slot_count - 1)
        sending = jnp.take(expert_produced, selector.reshape(-1), axis=0).reshape(
            ranks_total, per_peer, model_width
        )
        arrived = lax.all_to_all(sending, "ep", split_axis=0, concat_axis=0, tiled=True)
        flattened = arrived.reshape(ranks_total * per_peer, model_width)
        location = routes[batch_index] * per_peer + rank_in_block[batch_index]
        gathered = jnp.take(flattened, location.reshape(-1), axis=0).reshape(
            row_count, choose_count, model_width
        )
        weighted = jnp.sum(
            route_weight[batch_index][:, :, None] * gathered.astype(jnp.float32), axis=1
        )
        results.append((residual[batch_index].astype(jnp.float32) + weighted).astype(jnp.bfloat16))
    return jnp.stack(results, axis=0)


MESH = pl.DeviceIdType.MESH
TILE = 512


def dense_kernel(
    sizes, hidden_hbm, weight_hbm, routes_hbm, shares_hbm, residual_hbm, mixed_ref,
    hidden, weight, routes, shares, residual, produced,
    note_out, note_in, slot_of,
    core_out, core_in, core_kept, x_out, x_in, x_kept, z_out, z_in,
    load_sem, column_sem, note_send, note_recv, core_send, core_recv, x_send, x_recv, z_send, z_recv,
):
    ranks, batches, rows, chosen, slots, width = sizes
    both = batches * rows
    me = lax.axis_index("ep")
    core, x, z = lax.rem(me, 2), lax.rem(me // 2, 2), me // 4
    low, high = lax.rem(z, 2), z // 2
    sibling = me + 1 - 2 * core
    beside = me + 2 - 4 * x
    near = me + 4 - 8 * low
    far = me + 8 - 16 * high

    barrier = pltpu.get_barrier_semaphore()

    def greet(step, carry):
        pl.semaphore_signal(
            barrier, inc=1, device_id={"ep": lax.rem(me + step, ranks)}, device_id_type=MESH
        )
        return carry

    lax.fori_loop(1, ranks, greet, 0)

    loads = [
        pltpu.make_async_copy(routes_hbm, routes, load_sem.at[0]),
        pltpu.make_async_copy(shares_hbm, shares, load_sem.at[1]),
        pltpu.make_async_copy(hidden_hbm, hidden, load_sem.at[2]),
    ]
    columns = [
        pltpu.make_async_copy(
            weight_hbm.at[:, pl.ds(j * TILE, TILE)], weight.at[j], column_sem.at[j]
        )
        for j in range(width // TILE)
    ]
    residual_load = pltpu.make_async_copy(residual_hbm, residual, load_sem.at[3])
    for copy in loads + columns + [residual_load]:
        copy.start()

    loads[0].wait()
    loads[1].wait()
    given, named = [], []
    expert = lax.broadcasted_iota(jnp.int32, (ranks, chosen, rows), 0)
    for b in range(batches):
        hit = routes[b][None] == expert
        given.append(jnp.sum(jnp.where(hit, shares[b][None], 0.0), axis=1))
        named.append(jnp.sum(jnp.where(hit, 1.0, 0.0), axis=1))
    notes = jnp.concatenate(
        given + named + [jnp.zeros((ranks, 128 - 2 * both), jnp.float32)], axis=1
    )
    note_out[...] = notes.reshape(ranks, 1, 128)
    note_in[pl.ds(me, 1)] = note_out[pl.ds(me, 1)]

    pl.semaphore_wait(barrier, ranks - 1)

    def note_to(step):
        peer = lax.rem(me + step, ranks)
        return pltpu.make_async_remote_copy(
            src_ref=note_out.at[peer],
            dst_ref=note_in.at[me],
            send_sem=note_send.at[peer],
            recv_sem=note_recv.at[me],
            device_id={"ep": peer},
            device_id_type=MESH,
        )

    def note_from(step):
        peer = lax.rem(me + step, ranks)
        return pltpu.make_async_remote_copy(
            src_ref=note_out.at[peer],
            dst_ref=note_in.at[peer],
            send_sem=note_send.at[peer],
            recv_sem=note_recv.at[peer],
            device_id={"ep": peer},
            device_id_type=MESH,
        )

    def send_note(step, carry):
        note_to(step).start()
        return carry

    lax.fori_loop(1, ranks, send_note, 0)

    def produce(b, tiles):
        for j in tiles:
            if b == 0:
                columns[j].wait()
            produced[b, :, j * TILE : (j + 1) * TILE] = jnp.dot(
                hidden[b], weight[j], preferred_element_type=jnp.float32
            ).astype(jnp.bfloat16)

    tiles = width // TILE
    loads[2].wait()
    produce(0, range(tiles))

    def take_note(step, carry):
        note_from(step).wait_recv()
        return carry

    lax.fori_loop(1, ranks, take_note, 0)

    flags = note_in[...].reshape(ranks, 128)
    upper = lax.broadcasted_iota(jnp.int32, (128, 128), 0)
    lower = lax.broadcasted_iota(jnp.int32, (128, 128), 1)
    alike = (upper >= both) & (upper < 2 * both) & (lower >= both) & (lower < 2 * both)
    alike = alike & (upper // rows == lower // rows)
    ones = jnp.where(alike, 1.0, 0.0).astype(jnp.bfloat16)
    ahead = jnp.where(alike & (upper < lower), 1.0, 0.0).astype(jnp.bfloat16)
    packed = flags.astype(jnp.bfloat16)
    within = jnp.dot(packed, ahead, preferred_element_type=jnp.float32)
    counts = jnp.dot(packed, ones, preferred_element_type=jnp.float32).astype(jnp.bfloat16)
    earlier = lax.broadcasted_iota(jnp.int32, (ranks, ranks), 1) < lax.broadcasted_iota(
        jnp.int32, (ranks, ranks), 0
    )
    before = jnp.dot(
        jnp.where(earlier, 1.0, 0.0).astype(jnp.bfloat16), counts, preferred_element_type=jnp.float32
    )
    slot_of[...] = jnp.where(flags > 0.5, within + before, -1.0).reshape(ranks, 1, 128)

    lane = lax.broadcasted_iota(jnp.int32, (rows, 128), 1)
    row = lax.broadcasted_iota(jnp.int32, (rows, 128), 0)
    slot = lax.broadcasted_iota(jnp.int32, (4 * rows, slots), 1).astype(jnp.float32)

    def core_copy(i, b):
        return pltpu.make_async_remote_copy(
            src_ref=core_out.at[i, b], dst_ref=core_in.at[i, b],
            send_sem=core_send.at[i, b], recv_sem=core_recv.at[i, b],
            device_id={"ep": sibling}, device_id_type=MESH,
        )

    def x_copy(i, b):
        return pltpu.make_async_remote_copy(
            src_ref=x_out.at[i, b], dst_ref=x_in.at[i, b],
            send_sem=x_send.at[i, b], recv_sem=x_recv.at[i, b],
            device_id={"ep": beside}, device_id_type=MESH,
        )

    def z_copy(i, b):
        return pltpu.make_async_remote_copy(
            src_ref=z_out.at[i, b], dst_ref=z_in.at[i, b],
            send_sem=z_send.at[i, b], recv_sem=z_recv.at[i, b],
            device_id={"ep": far if i == 1 else near}, device_id_type=MESH,
        )

    def spread(i, b):
        plane = 2 * lax.rem(high + 1 - i // 2, 2) + lax.rem(low + 1 - i % 2, 2)
        factor, place = [], []
        for other_core in (1, 0):
            for other_x in (1, 0):
                c = lax.rem(core + other_core, 2)
                at_x = lax.rem(x + other_x, 2)
                owner = plane * 4 + at_x * 2 + c
                factor.append(
                    jnp.sum(
                        jnp.where(lane == row + b * rows, note_in[owner], 0.0), axis=1, keepdims=True
                    )
                )
                place.append(
                    jnp.sum(
                        jnp.where(lane == row + (both + b * rows), slot_of[owner], 0.0),
                        axis=1, keepdims=True,
                    )
                )
        scale = jnp.concatenate(factor, axis=0)
        spot = jnp.concatenate(place, axis=0)
        pick = jnp.where(spot == slot, 1.0, 0.0).astype(jnp.bfloat16)
        for j in range(tiles):
            cut = slice(j * TILE, (j + 1) * TILE)
            part = scale * jnp.dot(pick, produced[b, :, cut], preferred_element_type=jnp.float32)
            core_out[i, b, :, cut] = part[: 2 * rows].astype(jnp.bfloat16)
            core_kept[i, b, :, cut] = part[2 * rows :]
        core_copy(i, b).start()

    def over_cores(i, b):
        core_copy(i, b).wait_recv()
        total = core_kept[i, b] + core_in[i, b].astype(jnp.float32)
        x_out[i, b] = total[:rows].astype(jnp.bfloat16)
        x_kept[i, b] = total[rows:]
        x_copy(i, b).start()

    def over_x(i, b):
        x_copy(i, b).wait_recv()
        total = x_kept[i, b] + x_in[i, b].astype(jnp.float32)
        if i == 1:
            z_copy(0, b).wait_recv()
            total = total + z_in[0, b].astype(jnp.float32)
        if i < 3:
            z_out[i, b] = total.astype(jnp.bfloat16)
            z_copy(i, b).start()
        else:
            total = total + residual[b].astype(jnp.float32)
            z_copy(2, b).wait_recv()
            total = total + z_in[2, b].astype(jnp.float32)
            z_copy(1, b).wait_recv()
            mixed_ref[b] = (total + z_in[1, b].astype(jnp.float32)).astype(jnp.bfloat16)

    order = [(0, 0), (1, 0), (0, 1), (1, 1), (2, 0), (2, 1), (3, 0), (3, 1)]
    spread(*order[0])
    spread(*order[1])
    over_cores(*order[0])
    produce(1, range(tiles // 2))
    over_cores(*order[1])
    produce(1, range(tiles // 2, tiles))
    spread(*order[2])
    over_x(*order[0])
    spread(*order[3])
    over_cores(*order[2])
    spread(*order[4])
    over_cores(*order[3])
    over_x(*order[1])
    spread(*order[5])
    over_cores(*order[4])
    spread(*order[6])
    over_cores(*order[5])
    over_x(*order[2])
    spread(*order[7])
    over_cores(*order[6])
    over_cores(*order[7])
    residual_load.wait()
    for part in order[3:]:
        over_x(*part)

    for part in order:
        core_copy(*part).wait_send()
        x_copy(*part).wait_send()
        if part[0] < 3:
            z_copy(*part).wait_send()

    def note_left(step, carry):
        note_to(step).wait_send()
        return carry

    lax.fori_loop(1, ranks, note_left, 0)


def dense_shards(ranks, hidden, down_weight, routes, route_weight, residual):
    batches, rows, chosen = routes.shape
    slots, depth = hidden.shape[2:]
    width = down_weight.shape[2]
    both = batches * rows
    bf16, f32 = jnp.bfloat16, jnp.float32
    sizes = (ranks, batches, rows, chosen, slots, width)
    parts = 4
    return pl.pallas_call(
        functools.partial(dense_kernel, sizes),
        out_shape=jax.ShapeDtypeStruct((batches, rows, width), bf16),
        in_specs=[pl.BlockSpec(memory_space=pl.ANY)] * 5,
        out_specs=pl.BlockSpec(memory_space=pltpu.VMEM),
        scratch_shapes=[
            pltpu.VMEM((batches, slots, depth), bf16),
            pltpu.VMEM((width // TILE, depth, TILE), bf16),
            pltpu.VMEM((batches, chosen, rows), jnp.int32),
            pltpu.VMEM((batches, chosen, rows), f32),
            pltpu.VMEM((batches, rows, width), bf16),
            pltpu.VMEM((batches, slots, width), bf16),
            pltpu.VMEM((ranks, 1, 128), f32),
            pltpu.VMEM((ranks, 1, 128), f32),
            pltpu.VMEM((ranks, 1, 128), f32),
            pltpu.VMEM((parts, batches, 2 * rows, width), bf16),
            pltpu.VMEM((parts, batches, 2 * rows, width), bf16),
            pltpu.VMEM((parts, batches, 2 * rows, width), f32),
            pltpu.VMEM((parts, batches, rows, width), bf16),
            pltpu.VMEM((parts, batches, rows, width), bf16),
            pltpu.VMEM((parts, batches, rows, width), f32),
            pltpu.VMEM((3, batches, rows, width), bf16),
            pltpu.VMEM((3, batches, rows, width), bf16),
            pltpu.SemaphoreType.DMA((4,)),
            pltpu.SemaphoreType.DMA((width // TILE,)),
            pltpu.SemaphoreType.DMA((ranks,)),
            pltpu.SemaphoreType.DMA((ranks,)),
            pltpu.SemaphoreType.DMA((parts, batches)),
            pltpu.SemaphoreType.DMA((parts, batches)),
            pltpu.SemaphoreType.DMA((parts, batches)),
            pltpu.SemaphoreType.DMA((parts, batches)),
            pltpu.SemaphoreType.DMA((3, batches)),
            pltpu.SemaphoreType.DMA((3, batches)),
        ],
        compiler_params=pltpu.CompilerParams(
            collective_id=0, has_side_effects=True, vmem_limit_bytes=64 * 1024 * 1024 - 132 * 1024
        ),
    )(
        hidden.reshape(batches, slots, depth),
        down_weight.reshape(depth, width),
        jnp.swapaxes(routes, 1, 2),
        jnp.swapaxes(route_weight, 1, 2),
        residual,
    )


def solution(mesh):
    ranks = mesh.shape["ep"]
    in_specs = (
        P("dp", "ep", None, None),
        P("ep", None, None),
        P("dp", "ep", None),
        P("dp", "ep", None),
        P("dp", "ep", None),
    )
    out_specs = P("dp", "ep", None)

    def run(hidden, down_weight, routes, route_weight, residual):
        rows = routes.shape[1] // ranks
        batches = routes.shape[0] // mesh.shape["dp"]
        dense = ranks == 16 and rows % 16 == 0 and routes.shape[1] <= hidden.shape[2]
        dense = dense and batches == 2 and 2 * batches * rows <= 128
        body = functools.partial(dense_shards, ranks) if dense else shards
        return jax.shard_map(
            body, mesh=mesh, in_specs=in_specs, out_specs=out_specs, check_vma=False
        )(hidden, down_weight, routes, route_weight, residual)

    return run
```

```python
import functools
import math

import jax
import jax.numpy as jnp
from jax import lax
from jax.experimental import pallas as pl
from jax.experimental.pallas import tpu as pltpu
from jax.sharding import PartitionSpec as P


def shards(hidden, down_weight, routes, route_weight, residual):
    ranks_total = lax.axis_size("ep")
    batch_count = routes.shape[0]
    row_count = routes.shape[1]
    choose_count = routes.shape[2]
    slot_count = hidden.shape[2]
    per_peer = slot_count // ranks_total
    model_width = down_weight.shape[2]
    matrix = down_weight[0]
    labels = jnp.arange(ranks_total, dtype=jnp.int32)
    picked = jnp.sum((routes[:, :, :, None] == labels).astype(jnp.int32), axis=2, dtype=jnp.int32)
    rank_in_block = jnp.take_along_axis(
        jnp.cumsum(picked, axis=1, dtype=jnp.int32) - picked, routes, axis=2
    )
    loads_out = jnp.transpose(jnp.sum(picked, axis=1, dtype=jnp.int32))
    loads_in = lax.all_to_all(loads_out, "ep", split_axis=0, concat_axis=0, tiled=True)
    arriving = jnp.transpose(loads_in)
    offsets = jnp.cumsum(arriving, axis=1, dtype=jnp.int32) - arriving
    totals = jnp.sum(arriving, axis=1, dtype=jnp.int32)
    results = []
    for batch_index in range(batch_count):
        packed = hidden[batch_index, 0]
        block_size = math.gcd(slot_count, 128)

        def add_block(block_index, produced_in):
            begin_at = block_index * block_size
            segment = lax.dynamic_slice_in_dim(packed, begin_at, block_size, 0)
            product = jnp.dot(segment, matrix, preferred_element_type=jnp.float32).astype(
                jnp.bfloat16
            )
            return lax.dynamic_update_slice_in_dim(produced_in, product, begin_at, 0)

        block_count = (totals[batch_index] + block_size - 1) // block_size
        expert_produced = lax.fori_loop(
            0, block_count, add_block, jnp.zeros((slot_count, model_width), jnp.bfloat16)
        )
        selector = offsets[batch_index][:, None] + jnp.arange(per_peer, dtype=jnp.int32)[None, :]
        selector = jnp.minimum(selector, slot_count - 1)
        sending = jnp.take(expert_produced, selector.reshape(-1), axis=0).reshape(
            ranks_total, per_peer, model_width
        )
        arrived = lax.all_to_all(sending, "ep", split_axis=0, concat_axis=0, tiled=True)
        flattened = arrived.reshape(ranks_total * per_peer, model_width)
        location = routes[batch_index] * per_peer + rank_in_block[batch_index]
        gathered = jnp.take(flattened, location.reshape(-1), axis=0).reshape(
            row_count, choose_count, model_width
        )
        weighted = jnp.sum(
            route_weight[batch_index][:, :, None] * gathered.astype(jnp.float32), axis=1
        )
        results.append((residual[batch_index].astype(jnp.float32) + weighted).astype(jnp.bfloat16))
    return jnp.stack(results, axis=0)


MESH = pl.DeviceIdType.MESH
TILE = 512


def dense_kernel(
    sizes, hidden_hbm, weight_hbm, routes_hbm, shares_hbm, residual_hbm, mixed_ref,
    hidden, weight, routes, shares, residual, produced,
    note_out, note_in, slot_of,
    core_out, core_in, core_kept, x_out, x_in, x_kept, z_out, z_in,
    load_sem, column_sem, note_send, note_recv, core_send, core_recv, x_send, x_recv, z_send, z_recv,
):
    ranks, batches, rows, chosen, slots, width = sizes
    both = batches * rows
    me = lax.axis_index("ep")
    core, x, z = lax.rem(me, 2), lax.rem(me // 2, 2), me // 4
    low, high = lax.rem(z, 2), z // 2
    sibling = me + 1 - 2 * core
    beside = me + 2 - 4 * x
    near = me + 4 - 8 * low
    far = me + 8 - 16 * high

    barrier = pltpu.get_barrier_semaphore()

    def greet(step, carry):
        pl.semaphore_signal(
            barrier, inc=1, device_id={"ep": lax.rem(me + step, ranks)}, device_id_type=MESH
        )
        return carry

    lax.fori_loop(1, ranks, greet, 0)

    loads = [
        pltpu.make_async_copy(routes_hbm, routes, load_sem.at[0]),
        pltpu.make_async_copy(shares_hbm, shares, load_sem.at[1]),
        pltpu.make_async_copy(hidden_hbm, hidden, load_sem.at[2]),
    ]
    columns = [
        pltpu.make_async_copy(
            weight_hbm.at[:, pl.ds(j * TILE, TILE)], weight.at[j], column_sem.at[j]
        )
        for j in range(width // TILE)
    ]
    residual_load = pltpu.make_async_copy(residual_hbm, residual, load_sem.at[3])
    for copy in loads + columns + [residual_load]:
        copy.start()

    loads[0].wait()
    loads[1].wait()
    given, named = [], []
    expert = lax.broadcasted_iota(jnp.int32, (ranks, chosen, rows), 0)
    for b in range(batches):
        hit = routes[b][None] == expert
        given.append(jnp.sum(jnp.where(hit, shares[b][None], 0.0), axis=1))
        named.append(jnp.sum(jnp.where(hit, 1.0, 0.0), axis=1))
    notes = jnp.concatenate(
        given + named + [jnp.zeros((ranks, 128 - 2 * both), jnp.float32)], axis=1
    )
    note_out[...] = notes.reshape(ranks, 1, 128)
    note_in[pl.ds(me, 1)] = note_out[pl.ds(me, 1)]

    pl.semaphore_wait(barrier, ranks - 1)

    def note_to(step):
        peer = lax.rem(me + step, ranks)
        return pltpu.make_async_remote_copy(
            src_ref=note_out.at[peer],
            dst_ref=note_in.at[me],
            send_sem=note_send.at[peer],
            recv_sem=note_recv.at[me],
            device_id={"ep": peer},
            device_id_type=MESH,
        )

    def note_from(step):
        peer = lax.rem(me + step, ranks)
        return pltpu.make_async_remote_copy(
            src_ref=note_out.at[peer],
            dst_ref=note_in.at[peer],
            send_sem=note_send.at[peer],
            recv_sem=note_recv.at[peer],
            device_id={"ep": peer},
            device_id_type=MESH,
        )

    def send_note(step, carry):
        note_to(step).start()
        return carry

    lax.fori_loop(1, ranks, send_note, 0)

    def produce(b, tiles):
        for j in tiles:
            if b == 0:
                columns[j].wait()
            produced[b, :, j * TILE : (j + 1) * TILE] = jnp.dot(
                hidden[b], weight[j], preferred_element_type=jnp.float32
            ).astype(jnp.bfloat16)

    tiles = width // TILE
    loads[2].wait()
    produce(0, range(tiles))

    def take_note(step, carry):
        note_from(step).wait_recv()
        return carry

    lax.fori_loop(1, ranks, take_note, 0)

    flags = note_in[...].reshape(ranks, 128)
    upper = lax.broadcasted_iota(jnp.int32, (128, 128), 0)
    lower = lax.broadcasted_iota(jnp.int32, (128, 128), 1)
    alike = (upper >= both) & (upper < 2 * both) & (lower >= both) & (lower < 2 * both)
    alike = alike & (upper // rows == lower // rows)
    ones = jnp.where(alike, 1.0, 0.0).astype(jnp.bfloat16)
    ahead = jnp.where(alike & (upper < lower), 1.0, 0.0).astype(jnp.bfloat16)
    packed = flags.astype(jnp.bfloat16)
    within = jnp.dot(packed, ahead, preferred_element_type=jnp.float32)
    counts = jnp.dot(packed, ones, preferred_element_type=jnp.float32).astype(jnp.bfloat16)
    earlier = lax.broadcasted_iota(jnp.int32, (ranks, ranks), 1) < lax.broadcasted_iota(
        jnp.int32, (ranks, ranks), 0
    )
    before = jnp.dot(
        jnp.where(earlier, 1.0, 0.0).astype(jnp.bfloat16), counts, preferred_element_type=jnp.float32
    )
    slot_of[...] = jnp.where(flags > 0.5, within + before, -1.0).reshape(ranks, 1, 128)

    lane = lax.broadcasted_iota(jnp.int32, (rows, 128), 1)
    row = lax.broadcasted_iota(jnp.int32, (rows, 128), 0)
    slot = lax.broadcasted_iota(jnp.int32, (8 * rows, slots), 1).astype(jnp.float32)

    def core_copy(i, b):
        return pltpu.make_async_remote_copy(
            src_ref=core_out.at[i, b], dst_ref=core_in.at[i, b],
            send_sem=core_send.at[i, b], recv_sem=core_recv.at[i, b],
            device_id={"ep": sibling}, device_id_type=MESH,
        )

    def x_copy(i, b):
        return pltpu.make_async_remote_copy(
            src_ref=x_out.at[i, b], dst_ref=x_in.at[i, b],
            send_sem=x_send.at[i, b], recv_sem=x_recv.at[i, b],
            device_id={"ep": beside}, device_id_type=MESH,
        )

    def z_copy(i, b):
        return pltpu.make_async_remote_copy(
            src_ref=z_out.at[i, b], dst_ref=z_in.at[i, b],
            send_sem=z_send.at[i, b], recv_sem=z_recv.at[i, b],
            device_id={"ep": far if i == 1 else near}, device_id_type=MESH,
        )

    def spread(parts, b):
        factor, place = [], []
        for i in parts:
            plane = 2 * lax.rem(high + 1 - i // 2, 2) + lax.rem(low + 1 - i % 2, 2)
            for other_core in (1, 0):
                for other_x in (1, 0):
                    c = lax.rem(core + other_core, 2)
                    at_x = lax.rem(x + other_x, 2)
                    owner = plane * 4 + at_x * 2 + c
                    note, spot = note_in[owner], slot_of[owner]
                    factor.append(
                        jnp.sum(jnp.where(lane == row + b * rows, note, 0.0), axis=1, keepdims=True)
                    )
                    place.append(
                        jnp.sum(
                            jnp.where(lane == row + (both + b * rows), spot, 0.0),
                            axis=1, keepdims=True,
                        )
                    )
        scale = jnp.concatenate(factor, axis=0)
        pick = jnp.where(jnp.concatenate(place, axis=0) == slot, 1.0, 0.0).astype(jnp.bfloat16)
        for j in range(tiles):
            cut = slice(j * TILE, (j + 1) * TILE)
            part = scale * jnp.dot(pick, produced[b, :, cut], preferred_element_type=jnp.float32)
            for step, i in enumerate(parts):
                top = 4 * rows * step
                core_out[i, b, :, cut] = part[top : top + 2 * rows].astype(jnp.bfloat16)
                core_kept[i, b, :, cut] = part[top + 2 * rows : top + 4 * rows]
        for i in parts:
            core_copy(i, b).start()

    def over_cores(i, b):
        core_copy(i, b).wait_recv()
        total = core_kept[i, b] + core_in[i, b].astype(jnp.float32)
        x_out[i, b] = total[:rows].astype(jnp.bfloat16)
        x_kept[i, b] = total[rows:]
        x_copy(i, b).start()

    def over_x(i, b):
        x_copy(i, b).wait_recv()
        total = x_kept[i, b] + x_in[i, b].astype(jnp.float32)
        if i == 1:
            z_copy(0, b).wait_recv()
            total = total + z_in[0, b].astype(jnp.float32)
        if i < 3:
            z_out[i, b] = total.astype(jnp.bfloat16)
            z_copy(i, b).start()
        else:
            total = total + residual[b].astype(jnp.float32)
            z_copy(2, b).wait_recv()
            total = total + z_in[2, b].astype(jnp.float32)
            z_copy(1, b).wait_recv()
            mixed_ref[b] = (total + z_in[1, b].astype(jnp.float32)).astype(jnp.bfloat16)

    order = [(0, 0), (1, 0), (0, 1), (1, 1), (2, 0), (2, 1), (3, 0), (3, 1)]
    spread((0, 1), 0)
    produce(1, range(tiles // 2))
    over_cores(0, 0)
    over_cores(1, 0)
    produce(1, range(tiles // 2, tiles))
    spread((0, 1), 1)
    over_x(0, 0)
    spread((2, 3), 0)
    over_cores(0, 1)
    over_cores(1, 1)
    over_x(1, 0)
    spread((2, 3), 1)
    over_cores(2, 0)
    over_cores(2, 1)
    over_cores(3, 0)
    over_cores(3, 1)
    residual_load.wait()
    for part in order[2:]:
        over_x(*part)

    for part in order:
        core_copy(*part).wait_send()
        x_copy(*part).wait_send()
        if part[0] < 3:
            z_copy(*part).wait_send()

    def note_left(step, carry):
        note_to(step).wait_send()
        return carry

    lax.fori_loop(1, ranks, note_left, 0)


def dense_shards(ranks, hidden, down_weight, routes, route_weight, residual):
    batches, rows, chosen = routes.shape
    slots, depth = hidden.shape[2:]
    width = down_weight.shape[2]
    both = batches * rows
    bf16, f32 = jnp.bfloat16, jnp.float32
    sizes = (ranks, batches, rows, chosen, slots, width)
    parts = 4
    return pl.pallas_call(
        functools.partial(dense_kernel, sizes),
        out_shape=jax.ShapeDtypeStruct((batches, rows, width), bf16),
        in_specs=[pl.BlockSpec(memory_space=pl.ANY)] * 5,
        out_specs=pl.BlockSpec(memory_space=pltpu.VMEM),
        scratch_shapes=[
            pltpu.VMEM((batches, slots, depth), bf16),
            pltpu.VMEM((width // TILE, depth, TILE), bf16),
            pltpu.VMEM((batches, chosen, rows), jnp.int32),
            pltpu.VMEM((batches, chosen, rows), f32),
            pltpu.VMEM((batches, rows, width), bf16),
            pltpu.VMEM((batches, slots, width), bf16),
            pltpu.VMEM((ranks, 1, 128), f32),
            pltpu.VMEM((ranks, 1, 128), f32),
            pltpu.VMEM((ranks, 1, 128), f32),
            pltpu.VMEM((parts, batches, 2 * rows, width), bf16),
            pltpu.VMEM((parts, batches, 2 * rows, width), bf16),
            pltpu.VMEM((parts, batches, 2 * rows, width), f32),
            pltpu.VMEM((parts, batches, rows, width), bf16),
            pltpu.VMEM((parts, batches, rows, width), bf16),
            pltpu.VMEM((parts, batches, rows, width), f32),
            pltpu.VMEM((3, batches, rows, width), bf16),
            pltpu.VMEM((3, batches, rows, width), bf16),
            pltpu.SemaphoreType.DMA((4,)),
            pltpu.SemaphoreType.DMA((width // TILE,)),
            pltpu.SemaphoreType.DMA((ranks,)),
            pltpu.SemaphoreType.DMA((ranks,)),
            pltpu.SemaphoreType.DMA((parts, batches)),
            pltpu.SemaphoreType.DMA((parts, batches)),
            pltpu.SemaphoreType.DMA((parts, batches)),
            pltpu.SemaphoreType.DMA((parts, batches)),
            pltpu.SemaphoreType.DMA((3, batches)),
            pltpu.SemaphoreType.DMA((3, batches)),
        ],
        compiler_params=pltpu.CompilerParams(
            collective_id=0, has_side_effects=True, vmem_limit_bytes=48 * 1024 * 1024
        ),
    )(
        *[
            pltpu.with_memory_space_constraint(operand, pltpu.HBM)
            for operand in (
                hidden.reshape(batches, slots, depth),
                down_weight.reshape(depth, width),
                jnp.swapaxes(routes, 1, 2),
                jnp.swapaxes(route_weight, 1, 2),
                residual,
            )
        ]
    )


def solution(mesh):
    ranks = mesh.shape["ep"]
    in_specs = (
        P("dp", "ep", None, None),
        P("ep", None, None),
        P("dp", "ep", None),
        P("dp", "ep", None),
        P("dp", "ep", None),
    )
    out_specs = P("dp", "ep", None)

    def run(hidden, down_weight, routes, route_weight, residual):
        rows = routes.shape[1] // ranks
        batches = routes.shape[0] // mesh.shape["dp"]
        dense = ranks == 16 and rows % 16 == 0 and routes.shape[1] <= hidden.shape[2]
        dense = dense and batches == 2 and 2 * batches * rows <= 128
        body = functools.partial(dense_shards, ranks) if dense else shards
        return jax.shard_map(
            body, mesh=mesh, in_specs=in_specs, out_specs=out_specs, check_vma=False
        )(hidden, down_weight, routes, route_weight, residual)

    return run
```

```python
import functools
import math

import jax
import jax.numpy as jnp
from jax import lax
from jax.experimental import pallas as pl
from jax.experimental.pallas import tpu as pltpu
from jax.sharding import PartitionSpec as P


def shards(hidden, down_weight, routes, route_weight, residual):
    ranks_total = lax.axis_size("ep")
    batch_count = routes.shape[0]
    row_count = routes.shape[1]
    choose_count = routes.shape[2]
    slot_count = hidden.shape[2]
    per_peer = slot_count // ranks_total
    model_width = down_weight.shape[2]
    matrix = down_weight[0]
    labels = jnp.arange(ranks_total, dtype=jnp.int32)
    picked = jnp.sum((routes[:, :, :, None] == labels).astype(jnp.int32), axis=2, dtype=jnp.int32)
    rank_in_block = jnp.take_along_axis(
        jnp.cumsum(picked, axis=1, dtype=jnp.int32) - picked, routes, axis=2
    )
    loads_out = jnp.transpose(jnp.sum(picked, axis=1, dtype=jnp.int32))
    loads_in = lax.all_to_all(loads_out, "ep", split_axis=0, concat_axis=0, tiled=True)
    arriving = jnp.transpose(loads_in)
    offsets = jnp.cumsum(arriving, axis=1, dtype=jnp.int32) - arriving
    totals = jnp.sum(arriving, axis=1, dtype=jnp.int32)
    results = []
    for batch_index in range(batch_count):
        packed = hidden[batch_index, 0]
        block_size = math.gcd(slot_count, 128)

        def add_block(block_index, produced_in):
            begin_at = block_index * block_size
            segment = lax.dynamic_slice_in_dim(packed, begin_at, block_size, 0)
            product = jnp.dot(segment, matrix, preferred_element_type=jnp.float32).astype(
                jnp.bfloat16
            )
            return lax.dynamic_update_slice_in_dim(produced_in, product, begin_at, 0)

        block_count = (totals[batch_index] + block_size - 1) // block_size
        expert_produced = lax.fori_loop(
            0, block_count, add_block, jnp.zeros((slot_count, model_width), jnp.bfloat16)
        )
        selector = offsets[batch_index][:, None] + jnp.arange(per_peer, dtype=jnp.int32)[None, :]
        selector = jnp.minimum(selector, slot_count - 1)
        sending = jnp.take(expert_produced, selector.reshape(-1), axis=0).reshape(
            ranks_total, per_peer, model_width
        )
        arrived = lax.all_to_all(sending, "ep", split_axis=0, concat_axis=0, tiled=True)
        flattened = arrived.reshape(ranks_total * per_peer, model_width)
        location = routes[batch_index] * per_peer + rank_in_block[batch_index]
        gathered = jnp.take(flattened, location.reshape(-1), axis=0).reshape(
            row_count, choose_count, model_width
        )
        weighted = jnp.sum(
            route_weight[batch_index][:, :, None] * gathered.astype(jnp.float32), axis=1
        )
        results.append((residual[batch_index].astype(jnp.float32) + weighted).astype(jnp.bfloat16))
    return jnp.stack(results, axis=0)


MESH = pl.DeviceIdType.MESH
TILE = 512


def dense_kernel(
    sizes, hidden_hbm, weight_hbm, routes_hbm, shares_hbm, residual_hbm, mixed_ref,
    hidden, weight, routes, shares, residual, produced,
    note_out, note_in, slot_of,
    core_out, core_in, core_kept, x_out, x_in, x_kept, z_out, z_in,
    load_sem, column_sem, note_send, note_recv, core_send, core_recv, x_send, x_recv, z_send, z_recv,
):
    ranks, batches, rows, chosen, slots, width = sizes
    both = batches * rows
    me = lax.axis_index("ep")
    core, x, z = lax.rem(me, 2), lax.rem(me // 2, 2), me // 4
    low, high = lax.rem(z, 2), z // 2
    sibling = me + 1 - 2 * core
    beside = me + 2 - 4 * x
    near = me + 4 - 8 * low
    far = me + 8 - 16 * high

    barrier = pltpu.get_barrier_semaphore()

    def greet(step, carry):
        pl.semaphore_signal(
            barrier, inc=1, device_id={"ep": lax.rem(me + step, ranks)}, device_id_type=MESH
        )
        return carry

    lax.fori_loop(1, ranks, greet, 0)

    loads = [
        pltpu.make_async_copy(routes_hbm, routes, load_sem.at[0]),
        pltpu.make_async_copy(shares_hbm, shares, load_sem.at[1]),
        pltpu.make_async_copy(hidden_hbm, hidden, load_sem.at[2]),
    ]
    columns = [
        pltpu.make_async_copy(
            weight_hbm.at[:, pl.ds(j * TILE, TILE)], weight.at[j], column_sem.at[j]
        )
        for j in range(width // TILE)
    ]
    residual_load = pltpu.make_async_copy(residual_hbm, residual, load_sem.at[3])
    for copy in loads + columns + [residual_load]:
        copy.start()

    loads[0].wait()
    loads[1].wait()
    given, named = [], []
    expert = lax.broadcasted_iota(jnp.int32, (ranks, chosen, rows), 0)
    for b in range(batches):
        hit = routes[b][None] == expert
        given.append(jnp.sum(jnp.where(hit, shares[b][None], 0.0), axis=1))
        named.append(jnp.sum(jnp.where(hit, 1.0, 0.0), axis=1))
    notes = jnp.concatenate(
        given + named + [jnp.zeros((ranks, 128 - 2 * both), jnp.float32)], axis=1
    )
    note_out[...] = notes.reshape(ranks, 1, 128)
    note_in[pl.ds(me, 1)] = note_out[pl.ds(me, 1)]

    pl.semaphore_wait(barrier, ranks - 1)

    def note_to(step):
        peer = lax.rem(me + step, ranks)
        return pltpu.make_async_remote_copy(
            src_ref=note_out.at[peer],
            dst_ref=note_in.at[me],
            send_sem=note_send.at[peer],
            recv_sem=note_recv.at[me],
            device_id={"ep": peer},
            device_id_type=MESH,
        )

    def note_from(step):
        peer = lax.rem(me + step, ranks)
        return pltpu.make_async_remote_copy(
            src_ref=note_out.at[peer],
            dst_ref=note_in.at[peer],
            send_sem=note_send.at[peer],
            recv_sem=note_recv.at[peer],
            device_id={"ep": peer},
            device_id_type=MESH,
        )

    def send_note(step, carry):
        note_to(step).start()
        return carry

    lax.fori_loop(1, ranks, send_note, 0)

    def produce(b, tiles):
        for j in tiles:
            if b == 0:
                columns[j].wait()
            produced[b, :, j * TILE : (j + 1) * TILE] = jnp.dot(
                hidden[b], weight[j], preferred_element_type=jnp.float32
            ).astype(jnp.bfloat16)

    tiles = width // TILE
    loads[2].wait()
    produce(0, range(tiles))

    def take_note(step, carry):
        note_from(step).wait_recv()
        return carry

    lax.fori_loop(1, ranks, take_note, 0)

    flags = note_in[...].reshape(ranks, 128)
    upper = lax.broadcasted_iota(jnp.int32, (128, 128), 0)
    lower = lax.broadcasted_iota(jnp.int32, (128, 128), 1)
    alike = (upper >= both) & (upper < 2 * both) & (lower >= both) & (lower < 2 * both)
    alike = alike & (upper // rows == lower // rows)
    ones = jnp.where(alike, 1.0, 0.0).astype(jnp.bfloat16)
    ahead = jnp.where(alike & (upper < lower), 1.0, 0.0).astype(jnp.bfloat16)
    packed = flags.astype(jnp.bfloat16)
    within = jnp.dot(packed, ahead, preferred_element_type=jnp.float32)
    counts = jnp.dot(packed, ones, preferred_element_type=jnp.float32).astype(jnp.bfloat16)
    earlier = lax.broadcasted_iota(jnp.int32, (ranks, ranks), 1) < lax.broadcasted_iota(
        jnp.int32, (ranks, ranks), 0
    )
    before = jnp.dot(
        jnp.where(earlier, 1.0, 0.0).astype(jnp.bfloat16), counts, preferred_element_type=jnp.float32
    )
    slot_of[...] = jnp.where(flags > 0.5, within + before, -1.0).reshape(ranks, 1, 128)

    lane = lax.broadcasted_iota(jnp.int32, (rows, 128), 1)
    row = lax.broadcasted_iota(jnp.int32, (rows, 128), 0)
    slot = lax.broadcasted_iota(jnp.int32, (8 * rows, slots), 1).astype(jnp.float32)

    def core_copy(i, b):
        return pltpu.make_async_remote_copy(
            src_ref=core_out.at[i, b], dst_ref=core_in.at[i, b],
            send_sem=core_send.at[i, b], recv_sem=core_recv.at[i, b],
            device_id={"ep": sibling}, device_id_type=MESH,
        )

    def x_copy(i, b):
        return pltpu.make_async_remote_copy(
            src_ref=x_out.at[i, b], dst_ref=x_in.at[i, b],
            send_sem=x_send.at[i, b], recv_sem=x_recv.at[i, b],
            device_id={"ep": beside}, device_id_type=MESH,
        )

    def z_copy(i, b):
        return pltpu.make_async_remote_copy(
            src_ref=z_out.at[i, b], dst_ref=z_in.at[i, b],
            send_sem=z_send.at[i, b], recv_sem=z_recv.at[i, b],
            device_id={"ep": far if i == 1 else near}, device_id_type=MESH,
        )

    def spread(parts, b):
        factor, place = [], []
        for i in parts:
            plane = 2 * lax.rem(high + 1 - i // 2, 2) + lax.rem(low + 1 - i % 2, 2)
            for other_core in (1, 0):
                for other_x in (1, 0):
                    c = lax.rem(core + other_core, 2)
                    at_x = lax.rem(x + other_x, 2)
                    owner = plane * 4 + at_x * 2 + c
                    note, spot = note_in[owner], slot_of[owner]
                    factor.append(
                        jnp.sum(jnp.where(lane == row + b * rows, note, 0.0), axis=1, keepdims=True)
                    )
                    place.append(
                        jnp.sum(
                            jnp.where(lane == row + (both + b * rows), spot, 0.0),
                            axis=1, keepdims=True,
                        )
                    )
        scale = jnp.concatenate(factor, axis=0)
        pick = jnp.where(jnp.concatenate(place, axis=0) == slot, 1.0, 0.0).astype(jnp.bfloat16)
        for j in range(tiles):
            cut = slice(j * TILE, (j + 1) * TILE)
            part = scale * jnp.dot(pick, produced[b, :, cut], preferred_element_type=jnp.float32)
            for step, i in enumerate(parts):
                top = 4 * rows * step
                core_out[i, b, :, cut] = part[top : top + 2 * rows].astype(jnp.bfloat16)
                core_kept[i, b, :, cut] = part[top + 2 * rows : top + 4 * rows]
        for i in parts:
            core_copy(i, b).start()

    def over_cores(i, b):
        core_copy(i, b).wait_recv()
        total = core_kept[i, b] + core_in[i, b].astype(jnp.float32)
        x_out[i, b] = total[:rows].astype(jnp.bfloat16)
        x_kept[i, b] = total[rows:]

    def over_x(at):
        i, b = order[at]
        x_copy(i, b).wait_recv()
        total = x_kept[i, b] + x_in[i, b].astype(jnp.float32)
        if i == 1:
            if at + 2 < len(order):
                x_copy(*order[at + 2]).start()
            z_copy(0, b).wait_recv()
            total = total + z_in[0, b].astype(jnp.float32)
        if i < 3:
            z_out[i, b] = total.astype(jnp.bfloat16)
            z_copy(i, b).start()
        else:
            total = total + residual[b].astype(jnp.float32)
            z_copy(2, b).wait_recv()
            total = total + z_in[2, b].astype(jnp.float32)
            z_copy(1, b).wait_recv()
            mixed_ref[b] = (total + z_in[1, b].astype(jnp.float32)).astype(jnp.bfloat16)
        if i != 1 and at + 2 < len(order):
            x_copy(*order[at + 2]).start()

    order = [(0, 0), (1, 0), (0, 1), (1, 1), (2, 0), (2, 1), (3, 0), (3, 1)]
    spread((0, 1), 0)
    produce(1, range(tiles // 2))
    over_cores(0, 0)
    x_copy(0, 0).start()
    over_cores(1, 0)
    x_copy(1, 0).start()
    produce(1, range(tiles // 2, tiles))
    spread((0, 1), 1)
    over_cores(0, 1)
    over_x(0)
    over_cores(1, 1)
    spread((2, 3), 0)
    over_x(1)
    spread((2, 3), 1)
    over_cores(2, 0)
    over_cores(2, 1)
    over_x(2)
    over_cores(3, 0)
    over_cores(3, 1)
    residual_load.wait()
    for at in range(3, len(order)):
        over_x(at)

    for part in order:
        core_copy(*part).wait_send()
        x_copy(*part).wait_send()
        if part[0] < 3:
            z_copy(*part).wait_send()

    def note_left(step, carry):
        note_to(step).wait_send()
        return carry

    lax.fori_loop(1, ranks, note_left, 0)


def dense_shards(ranks, hidden, down_weight, routes, route_weight, residual):
    batches, rows, chosen = routes.shape
    slots, depth = hidden.shape[2:]
    width = down_weight.shape[2]
    both = batches * rows
    bf16, f32 = jnp.bfloat16, jnp.float32
    sizes = (ranks, batches, rows, chosen, slots, width)
    parts = 4
    return pl.pallas_call(
        functools.partial(dense_kernel, sizes),
        out_shape=jax.ShapeDtypeStruct((batches, rows, width), bf16),
        in_specs=[pl.BlockSpec(memory_space=pl.ANY)] * 5,
        out_specs=pl.BlockSpec(memory_space=pltpu.VMEM),
        scratch_shapes=[
            pltpu.VMEM((batches, slots, depth), bf16),
            pltpu.VMEM((width // TILE, depth, TILE), bf16),
            pltpu.VMEM((batches, chosen, rows), jnp.int32),
            pltpu.VMEM((batches, chosen, rows), f32),
            pltpu.VMEM((batches, rows, width), bf16),
            pltpu.VMEM((batches, slots, width), bf16),
            pltpu.VMEM((ranks, 1, 128), f32),
            pltpu.VMEM((ranks, 1, 128), f32),
            pltpu.VMEM((ranks, 1, 128), f32),
            pltpu.VMEM((parts, batches, 2 * rows, width), bf16),
            pltpu.VMEM((parts, batches, 2 * rows, width), bf16),
            pltpu.VMEM((parts, batches, 2 * rows, width), f32),
            pltpu.VMEM((parts, batches, rows, width), bf16),
            pltpu.VMEM((parts, batches, rows, width), bf16),
            pltpu.VMEM((parts, batches, rows, width), f32),
            pltpu.VMEM((3, batches, rows, width), bf16),
            pltpu.VMEM((3, batches, rows, width), bf16),
            pltpu.SemaphoreType.DMA((4,)),
            pltpu.SemaphoreType.DMA((width // TILE,)),
            pltpu.SemaphoreType.DMA((ranks,)),
            pltpu.SemaphoreType.DMA((ranks,)),
            pltpu.SemaphoreType.DMA((parts, batches)),
            pltpu.SemaphoreType.DMA((parts, batches)),
            pltpu.SemaphoreType.DMA((parts, batches)),
            pltpu.SemaphoreType.DMA((parts, batches)),
            pltpu.SemaphoreType.DMA((3, batches)),
            pltpu.SemaphoreType.DMA((3, batches)),
        ],
        compiler_params=pltpu.CompilerParams(
            collective_id=0, has_side_effects=True, vmem_limit_bytes=48 * 1024 * 1024
        ),
    )(
        *[
            pltpu.with_memory_space_constraint(operand, pltpu.HBM)
            for operand in (
                hidden.reshape(batches, slots, depth),
                down_weight.reshape(depth, width),
                jnp.swapaxes(routes, 1, 2),
                jnp.swapaxes(route_weight, 1, 2),
                residual,
            )
        ]
    )


def solution(mesh):
    ranks = mesh.shape["ep"]
    in_specs = (
        P("dp", "ep", None, None),
        P("ep", None, None),
        P("dp", "ep", None),
        P("dp", "ep", None),
        P("dp", "ep", None),
    )
    out_specs = P("dp", "ep", None)

    def run(hidden, down_weight, routes, route_weight, residual):
        rows = routes.shape[1] // ranks
        batches = routes.shape[0] // mesh.shape["dp"]
        dense = ranks == 16 and rows % 16 == 0 and routes.shape[1] <= hidden.shape[2]
        dense = dense and batches == 2 and 2 * batches * rows <= 128
        body = functools.partial(dense_shards, ranks) if dense else shards
        return jax.shard_map(
            body, mesh=mesh, in_specs=in_specs, out_specs=out_specs, check_vma=False
        )(hidden, down_weight, routes, route_weight, residual)

    return run
```

```python
import functools
import math

import jax
import jax.numpy as jnp
from jax import lax
from jax.experimental import pallas as pl
from jax.experimental.pallas import tpu as pltpu
from jax.sharding import PartitionSpec as P


def shards(hidden, down_weight, routes, route_weight, residual):
    ranks_total = lax.axis_size("ep")
    batch_count = routes.shape[0]
    row_count = routes.shape[1]
    choose_count = routes.shape[2]
    slot_count = hidden.shape[2]
    per_peer = slot_count // ranks_total
    model_width = down_weight.shape[2]
    matrix = down_weight[0]
    labels = jnp.arange(ranks_total, dtype=jnp.int32)
    picked = jnp.sum((routes[:, :, :, None] == labels).astype(jnp.int32), axis=2, dtype=jnp.int32)
    rank_in_block = jnp.take_along_axis(
        jnp.cumsum(picked, axis=1, dtype=jnp.int32) - picked, routes, axis=2
    )
    loads_out = jnp.transpose(jnp.sum(picked, axis=1, dtype=jnp.int32))
    loads_in = lax.all_to_all(loads_out, "ep", split_axis=0, concat_axis=0, tiled=True)
    arriving = jnp.transpose(loads_in)
    offsets = jnp.cumsum(arriving, axis=1, dtype=jnp.int32) - arriving
    totals = jnp.sum(arriving, axis=1, dtype=jnp.int32)
    results = []
    for batch_index in range(batch_count):
        packed = hidden[batch_index, 0]
        block_size = math.gcd(slot_count, 128)

        def add_block(block_index, produced_in):
            begin_at = block_index * block_size
            segment = lax.dynamic_slice_in_dim(packed, begin_at, block_size, 0)
            product = jnp.dot(segment, matrix, preferred_element_type=jnp.float32).astype(
                jnp.bfloat16
            )
            return lax.dynamic_update_slice_in_dim(produced_in, product, begin_at, 0)

        block_count = (totals[batch_index] + block_size - 1) // block_size
        expert_produced = lax.fori_loop(
            0, block_count, add_block, jnp.zeros((slot_count, model_width), jnp.bfloat16)
        )
        selector = offsets[batch_index][:, None] + jnp.arange(per_peer, dtype=jnp.int32)[None, :]
        selector = jnp.minimum(selector, slot_count - 1)
        sending = jnp.take(expert_produced, selector.reshape(-1), axis=0).reshape(
            ranks_total, per_peer, model_width
        )
        arrived = lax.all_to_all(sending, "ep", split_axis=0, concat_axis=0, tiled=True)
        flattened = arrived.reshape(ranks_total * per_peer, model_width)
        location = routes[batch_index] * per_peer + rank_in_block[batch_index]
        gathered = jnp.take(flattened, location.reshape(-1), axis=0).reshape(
            row_count, choose_count, model_width
        )
        weighted = jnp.sum(
            route_weight[batch_index][:, :, None] * gathered.astype(jnp.float32), axis=1
        )
        results.append((residual[batch_index].astype(jnp.float32) + weighted).astype(jnp.bfloat16))
    return jnp.stack(results, axis=0)


MESH = pl.DeviceIdType.MESH
TILE = 512


def dense_kernel(
    sizes, hidden_hbm, weight_hbm, routes_hbm, shares_hbm, residual_hbm, mixed_ref,
    hidden, weight, routes, shares, residual, produced,
    note_out, note_in, slot_of,
    core_out, core_in, core_kept, x_out, x_in, x_kept, z_out, z_in, near_out, near_in, near_kept,
    load_sem, column_sem, note_send, note_recv, core_send, core_recv, x_send, x_recv, z_send, z_recv,
    near_send, near_recv,
):
    ranks, batches, rows, chosen, slots, width = sizes
    both = batches * rows
    me = lax.axis_index("ep")
    core, x, z = lax.rem(me, 2), lax.rem(me // 2, 2), me // 4
    low, high = lax.rem(z, 2), z // 2
    sibling = me + 1 - 2 * core
    beside = me + 2 - 4 * x
    near = me + 4 - 8 * low
    far = me + 8 - 16 * high

    barrier = pltpu.get_barrier_semaphore()

    def greet(step, carry):
        pl.semaphore_signal(
            barrier, inc=1, device_id={"ep": lax.rem(me + step, ranks)}, device_id_type=MESH
        )
        return carry

    lax.fori_loop(1, ranks, greet, 0)

    loads = [
        pltpu.make_async_copy(routes_hbm, routes, load_sem.at[0]),
        pltpu.make_async_copy(shares_hbm, shares, load_sem.at[1]),
        pltpu.make_async_copy(hidden_hbm, hidden, load_sem.at[2]),
    ]
    columns = [
        pltpu.make_async_copy(
            weight_hbm.at[:, pl.ds(j * TILE, TILE)], weight.at[j], column_sem.at[j]
        )
        for j in range(width // TILE)
    ]
    residual_load = pltpu.make_async_copy(residual_hbm, residual, load_sem.at[3])
    for copy in loads + columns + [residual_load]:
        copy.start()

    loads[0].wait()
    loads[1].wait()
    given, named = [], []
    expert = lax.broadcasted_iota(jnp.int32, (ranks, chosen, rows), 0)
    for b in range(batches):
        hit = routes[b][None] == expert
        given.append(jnp.sum(jnp.where(hit, shares[b][None], 0.0), axis=1))
        named.append(jnp.sum(jnp.where(hit, 1.0, 0.0), axis=1))
    notes = jnp.concatenate(
        given + named + [jnp.zeros((ranks, 128 - 2 * both), jnp.float32)], axis=1
    )
    note_out[...] = notes.reshape(ranks, 1, 128)
    note_in[pl.ds(me, 1)] = note_out[pl.ds(me, 1)]

    pl.semaphore_wait(barrier, ranks - 1)

    def note_to(step):
        peer = lax.rem(me + step, ranks)
        return pltpu.make_async_remote_copy(
            src_ref=note_out.at[peer],
            dst_ref=note_in.at[me],
            send_sem=note_send.at[peer],
            recv_sem=note_recv.at[me],
            device_id={"ep": peer},
            device_id_type=MESH,
        )

    def note_from(step):
        peer = lax.rem(me + step, ranks)
        return pltpu.make_async_remote_copy(
            src_ref=note_out.at[peer],
            dst_ref=note_in.at[peer],
            send_sem=note_send.at[peer],
            recv_sem=note_recv.at[peer],
            device_id={"ep": peer},
            device_id_type=MESH,
        )

    def send_note(step, carry):
        note_to(step).start()
        return carry

    lax.fori_loop(1, ranks, send_note, 0)

    def produce(b, tiles):
        for j in tiles:
            if b == 0:
                columns[j].wait()
            produced[b, :, j * TILE : (j + 1) * TILE] = jnp.dot(
                hidden[b], weight[j], preferred_element_type=jnp.float32
            ).astype(jnp.bfloat16)

    tiles = width // TILE
    loads[2].wait()
    produce(0, range(tiles))
    produce(1, range(tiles))

    def take_note(step, carry):
        note_from(step).wait_recv()
        return carry

    lax.fori_loop(1, ranks, take_note, 0)

    flags = note_in[...].reshape(ranks, 128)
    upper = lax.broadcasted_iota(jnp.int32, (128, 128), 0)
    lower = lax.broadcasted_iota(jnp.int32, (128, 128), 1)
    alike = (upper >= both) & (upper < 2 * both) & (lower >= both) & (lower < 2 * both)
    alike = alike & (upper // rows == lower // rows)
    ones = jnp.where(alike, 1.0, 0.0).astype(jnp.bfloat16)
    ahead = jnp.where(alike & (upper < lower), 1.0, 0.0).astype(jnp.bfloat16)
    packed = flags.astype(jnp.bfloat16)
    within = jnp.dot(packed, ahead, preferred_element_type=jnp.float32)
    counts = jnp.dot(packed, ones, preferred_element_type=jnp.float32).astype(jnp.bfloat16)
    earlier = lax.broadcasted_iota(jnp.int32, (ranks, ranks), 1) < lax.broadcasted_iota(
        jnp.int32, (ranks, ranks), 0
    )
    before = jnp.dot(
        jnp.where(earlier, 1.0, 0.0).astype(jnp.bfloat16), counts, preferred_element_type=jnp.float32
    )
    slot_of[...] = jnp.where(flags > 0.5, within + before, -1.0).reshape(ranks, 1, 128)

    lane = lax.broadcasted_iota(jnp.int32, (rows, 128), 1)
    row = lax.broadcasted_iota(jnp.int32, (rows, 128), 0)
    slot = lax.broadcasted_iota(jnp.int32, (8 * rows, slots), 1).astype(jnp.float32)

    def core_copy(i, b):
        return pltpu.make_async_remote_copy(
            src_ref=core_out.at[i, b], dst_ref=core_in.at[i, b],
            send_sem=core_send.at[i, b], recv_sem=core_recv.at[i, b],
            device_id={"ep": sibling}, device_id_type=MESH,
        )

    def x_copy(i, b):
        return pltpu.make_async_remote_copy(
            src_ref=x_out.at[i, b], dst_ref=x_in.at[i, b],
            send_sem=x_send.at[i, b], recv_sem=x_recv.at[i, b],
            device_id={"ep": beside}, device_id_type=MESH,
        )

    def z_copy(i, b):
        return pltpu.make_async_remote_copy(
            src_ref=z_out.at[i, b], dst_ref=z_in.at[i, b],
            send_sem=z_send.at[i, b], recv_sem=z_recv.at[i, b],
            device_id={"ep": far if i == 1 else near}, device_id_type=MESH,
        )

    def spread(parts, b):
        factor, place = [], []
        for i in parts:
            plane = 2 * lax.rem(high + 1 - i // 2, 2) + lax.rem(low + 1 - i % 2, 2)
            for other_core in (1, 0):
                for other_x in (1, 0):
                    c = lax.rem(core + other_core, 2)
                    at_x = lax.rem(x + other_x, 2)
                    owner = plane * 4 + at_x * 2 + c
                    note, spot = note_in[owner], slot_of[owner]
                    factor.append(
                        jnp.sum(jnp.where(lane == row + b * rows, note, 0.0), axis=1, keepdims=True)
                    )
                    place.append(
                        jnp.sum(
                            jnp.where(lane == row + (both + b * rows), spot, 0.0),
                            axis=1, keepdims=True,
                        )
                    )
        scale = jnp.concatenate(factor, axis=0)
        pick = jnp.where(jnp.concatenate(place, axis=0) == slot, 1.0, 0.0).astype(jnp.bfloat16)
        for j in range(tiles):
            cut = slice(j * TILE, (j + 1) * TILE)
            part = scale * jnp.dot(pick, produced[b, :, cut], preferred_element_type=jnp.float32)
            for step, i in enumerate(parts):
                top = 4 * rows * step
                core_out[i, b, :, cut] = part[top : top + 2 * rows].astype(jnp.bfloat16)
                core_kept[i, b, :, cut] = part[top + 2 * rows : top + 4 * rows]
        for i in parts:
            core_copy(i, b).start()

    def near_copy(k):
        return pltpu.make_async_remote_copy(
            src_ref=near_out.at[k], dst_ref=near_in.at[k],
            send_sem=near_send.at[k], recv_sem=near_recv.at[k],
            device_id={"ep": near}, device_id_type=MESH,
        )

    def over_cores(i, b):
        core_copy(i, b).wait_recv()
        total = core_kept[i, b] + core_in[i, b].astype(jnp.float32)
        if b == 0:
            x_out[i, b] = total[:rows].astype(jnp.bfloat16)
            x_kept[i, b] = total[rows:]
            x_copy(i, b).start()
        elif i % 2 == 0:
            near_out[i // 2] = total.astype(jnp.bfloat16)
            near_copy(i // 2).start()
        else:
            near_kept[i // 2] = total

    def over_near(i):
        near_copy(i // 2).wait_recv()
        total = near_kept[i // 2] + near_in[i // 2].astype(jnp.float32)
        x_out[i, 1] = total[:rows].astype(jnp.bfloat16)
        x_kept[i, 1] = total[rows:]
        x_copy(i, 1).start()

    def over_x(i, b):
        x_copy(i, b).wait_recv()
        total = x_kept[i, b] + x_in[i, b].astype(jnp.float32)
        if i == 1 and b == 0:
            z_copy(0, b).wait_recv()
            total = total + z_in[0, b].astype(jnp.float32)
        if i < 3:
            z_out[i, b] = total.astype(jnp.bfloat16)
            z_copy(i, b).start()
        else:
            total = total + residual[b].astype(jnp.float32)
            if b == 0:
                z_copy(2, b).wait_recv()
                total = total + z_in[2, b].astype(jnp.float32)
            z_copy(1, b).wait_recv()
            mixed_ref[b] = (total + z_in[1, b].astype(jnp.float32)).astype(jnp.bfloat16)

    spread((0, 1), 0)
    spread((0, 1), 1)
    over_cores(0, 0)
    over_cores(0, 1)
    over_cores(1, 0)
    over_cores(1, 1)
    spread((2, 3), 0)
    over_cores(2, 0)
    over_x(0, 0)
    over_cores(3, 0)
    spread((2, 3), 1)
    over_near(1)
    over_cores(2, 1)
    over_cores(3, 1)
    over_x(1, 0)
    over_x(2, 0)
    over_x(1, 1)
    over_near(3)
    residual_load.wait()
    over_x(3, 0)
    over_x(3, 1)

    for i in range(4):
        for b in range(batches):
            core_copy(i, b).wait_send()
        x_copy(i, 0).wait_send()
    for k in range(2):
        near_copy(k).wait_send()
        x_copy(2 * k + 1, 1).wait_send()
    for i in range(3):
        z_copy(i, 0).wait_send()
    z_copy(1, 1).wait_send()

    def note_left(step, carry):
        note_to(step).wait_send()
        return carry

    lax.fori_loop(1, ranks, note_left, 0)


def dense_shards(ranks, hidden, down_weight, routes, route_weight, residual):
    batches, rows, chosen = routes.shape
    slots, depth = hidden.shape[2:]
    width = down_weight.shape[2]
    both = batches * rows
    bf16, f32 = jnp.bfloat16, jnp.float32
    sizes = (ranks, batches, rows, chosen, slots, width)
    parts = 4
    return pl.pallas_call(
        functools.partial(dense_kernel, sizes),
        out_shape=jax.ShapeDtypeStruct((batches, rows, width), bf16),
        in_specs=[pl.BlockSpec(memory_space=pl.ANY)] * 5,
        out_specs=pl.BlockSpec(memory_space=pltpu.VMEM),
        scratch_shapes=[
            pltpu.VMEM((batches, slots, depth), bf16),
            pltpu.VMEM((width // TILE, depth, TILE), bf16),
            pltpu.VMEM((batches, chosen, rows), jnp.int32),
            pltpu.VMEM((batches, chosen, rows), f32),
            pltpu.VMEM((batches, rows, width), bf16),
            pltpu.VMEM((batches, slots, width), bf16),
            pltpu.VMEM((ranks, 1, 128), f32),
            pltpu.VMEM((ranks, 1, 128), f32),
            pltpu.VMEM((ranks, 1, 128), f32),
            pltpu.VMEM((parts, batches, 2 * rows, width), bf16),
            pltpu.VMEM((parts, batches, 2 * rows, width), bf16),
            pltpu.VMEM((parts, batches, 2 * rows, width), f32),
            pltpu.VMEM((parts, batches, rows, width), bf16),
            pltpu.VMEM((parts, batches, rows, width), bf16),
            pltpu.VMEM((parts, batches, rows, width), f32),
            pltpu.VMEM((3, batches, rows, width), bf16),
            pltpu.VMEM((3, batches, rows, width), bf16),
            pltpu.VMEM((2, 2 * rows, width), bf16),
            pltpu.VMEM((2, 2 * rows, width), bf16),
            pltpu.VMEM((2, 2 * rows, width), f32),
            pltpu.SemaphoreType.DMA((4,)),
            pltpu.SemaphoreType.DMA((width // TILE,)),
            pltpu.SemaphoreType.DMA((ranks,)),
            pltpu.SemaphoreType.DMA((ranks,)),
            pltpu.SemaphoreType.DMA((parts, batches)),
            pltpu.SemaphoreType.DMA((parts, batches)),
            pltpu.SemaphoreType.DMA((parts, batches)),
            pltpu.SemaphoreType.DMA((parts, batches)),
            pltpu.SemaphoreType.DMA((3, batches)),
            pltpu.SemaphoreType.DMA((3, batches)),
            pltpu.SemaphoreType.DMA((2,)),
            pltpu.SemaphoreType.DMA((2,)),
        ],
        compiler_params=pltpu.CompilerParams(
            collective_id=0, has_side_effects=True, vmem_limit_bytes=48 * 1024 * 1024
        ),
    )(
        *[
            pltpu.with_memory_space_constraint(operand, pltpu.HBM)
            for operand in (
                hidden.reshape(batches, slots, depth),
                down_weight.reshape(depth, width),
                jnp.swapaxes(routes, 1, 2),
                jnp.swapaxes(route_weight, 1, 2),
                residual,
            )
        ]
    )


def solution(mesh):
    ranks = mesh.shape["ep"]
    in_specs = (
        P("dp", "ep", None, None),
        P("ep", None, None),
        P("dp", "ep", None),
        P("dp", "ep", None),
        P("dp", "ep", None),
    )
    out_specs = P("dp", "ep", None)

    def run(hidden, down_weight, routes, route_weight, residual):
        rows = routes.shape[1] // ranks
        batches = routes.shape[0] // mesh.shape["dp"]
        dense = ranks == 16 and rows % 16 == 0 and routes.shape[1] <= hidden.shape[2]
        dense = dense and batches == 2 and 2 * batches * rows <= 128
        body = functools.partial(dense_shards, ranks) if dense else shards
        return jax.shard_map(
            body, mesh=mesh, in_specs=in_specs, out_specs=out_specs, check_vma=False
        )(hidden, down_weight, routes, route_weight, residual)

    return run
```

```python
import functools
import math

import jax
import jax.numpy as jnp
from jax import lax
from jax.experimental import pallas as pl
from jax.experimental.pallas import tpu as pltpu
from jax.sharding import PartitionSpec as P


def shards(hidden, down_weight, routes, route_weight, residual):
    ranks_total = lax.axis_size("ep")
    batch_count = routes.shape[0]
    row_count = routes.shape[1]
    choose_count = routes.shape[2]
    slot_count = hidden.shape[2]
    per_peer = slot_count // ranks_total
    model_width = down_weight.shape[2]
    matrix = down_weight[0]
    labels = jnp.arange(ranks_total, dtype=jnp.int32)
    picked = jnp.sum((routes[:, :, :, None] == labels).astype(jnp.int32), axis=2, dtype=jnp.int32)
    rank_in_block = jnp.take_along_axis(
        jnp.cumsum(picked, axis=1, dtype=jnp.int32) - picked, routes, axis=2
    )
    loads_out = jnp.transpose(jnp.sum(picked, axis=1, dtype=jnp.int32))
    loads_in = lax.all_to_all(loads_out, "ep", split_axis=0, concat_axis=0, tiled=True)
    arriving = jnp.transpose(loads_in)
    offsets = jnp.cumsum(arriving, axis=1, dtype=jnp.int32) - arriving
    totals = jnp.sum(arriving, axis=1, dtype=jnp.int32)
    results = []
    for batch_index in range(batch_count):
        packed = hidden[batch_index, 0]
        block_size = math.gcd(slot_count, 128)

        def add_block(block_index, produced_in):
            begin_at = block_index * block_size
            segment = lax.dynamic_slice_in_dim(packed, begin_at, block_size, 0)
            product = jnp.dot(segment, matrix, preferred_element_type=jnp.float32).astype(
                jnp.bfloat16
            )
            return lax.dynamic_update_slice_in_dim(produced_in, product, begin_at, 0)

        block_count = (totals[batch_index] + block_size - 1) // block_size
        expert_produced = lax.fori_loop(
            0, block_count, add_block, jnp.zeros((slot_count, model_width), jnp.bfloat16)
        )
        selector = offsets[batch_index][:, None] + jnp.arange(per_peer, dtype=jnp.int32)[None, :]
        selector = jnp.minimum(selector, slot_count - 1)
        sending = jnp.take(expert_produced, selector.reshape(-1), axis=0).reshape(
            ranks_total, per_peer, model_width
        )
        arrived = lax.all_to_all(sending, "ep", split_axis=0, concat_axis=0, tiled=True)
        flattened = arrived.reshape(ranks_total * per_peer, model_width)
        location = routes[batch_index] * per_peer + rank_in_block[batch_index]
        gathered = jnp.take(flattened, location.reshape(-1), axis=0).reshape(
            row_count, choose_count, model_width
        )
        weighted = jnp.sum(
            route_weight[batch_index][:, :, None] * gathered.astype(jnp.float32), axis=1
        )
        results.append((residual[batch_index].astype(jnp.float32) + weighted).astype(jnp.bfloat16))
    return jnp.stack(results, axis=0)


MESH = pl.DeviceIdType.MESH
TILE = 512


def dense_kernel(
    sizes, hidden_hbm, weight_hbm, routes_hbm, shares_hbm, residual_hbm, mixed_ref,
    hidden, weight, routes, shares, residual, produced,
    note_out, note_in, slot_of,
    core_out, core_in, core_kept, x_out, x_in, x_kept, z_out, z_in, near_out, near_in, near_kept,
    side_out, side_in, side_kept, far_out, far_in,
    load_sem, column_sem, note_send, note_recv, core_send, core_recv, x_send, x_recv, z_send, z_recv,
    near_send, near_recv, side_send, side_recv, far_send, far_recv,
):
    ranks, batches, rows, chosen, slots, width = sizes
    both = batches * rows
    me = lax.axis_index("ep")
    core, x, z = lax.rem(me, 2), lax.rem(me // 2, 2), me // 4
    low, high = lax.rem(z, 2), z // 2
    sibling = me + 1 - 2 * core
    beside = me + 2 - 4 * x
    near = me + 4 - 8 * low
    far = me + 8 - 16 * high

    barrier = pltpu.get_barrier_semaphore()

    turn = 2 * (me // (ranks // 2)) - 1

    def peer_of(step):
        return lax.rem(2 * ranks - 1 - me + turn * step, ranks)

    def greet(step, carry):
        peer = peer_of(step)

        @pl.when(peer != me)
        def _():
            pl.semaphore_signal(barrier, inc=1, device_id={"ep": peer}, device_id_type=MESH)

        return carry

    lax.fori_loop(0, ranks, greet, 0)

    loads = [
        pltpu.make_async_copy(routes_hbm, routes, load_sem.at[0]),
        pltpu.make_async_copy(shares_hbm, shares, load_sem.at[1]),
        pltpu.make_async_copy(hidden_hbm, hidden, load_sem.at[2]),
    ]
    columns = [
        pltpu.make_async_copy(
            weight_hbm.at[:, pl.ds(j * TILE, TILE)], weight.at[j], column_sem.at[j]
        )
        for j in range(width // TILE)
    ]
    residual_load = pltpu.make_async_copy(residual_hbm, residual, load_sem.at[3])
    for copy in loads + columns + [residual_load]:
        copy.start()

    loads[0].wait()
    loads[1].wait()
    given, named = [], []
    expert = lax.broadcasted_iota(jnp.int32, (ranks, chosen, rows), 0)
    for b in range(batches):
        hit = routes[b][None] == expert
        given.append(jnp.sum(jnp.where(hit, shares[b][None], 0.0), axis=1))
        named.append(jnp.sum(jnp.where(hit, 1.0, 0.0), axis=1))
    notes = jnp.concatenate(
        given + named + [jnp.zeros((ranks, 128 - 2 * both), jnp.float32)], axis=1
    )
    note_out[...] = notes.reshape(ranks, 1, 128)
    note_in[pl.ds(me, 1)] = note_out[pl.ds(me, 1)]

    pl.semaphore_wait(barrier, ranks - 1)

    def note_to(peer):
        return pltpu.make_async_remote_copy(
            src_ref=note_out.at[peer],
            dst_ref=note_in.at[me],
            send_sem=note_send.at[peer],
            recv_sem=note_recv.at[me],
            device_id={"ep": peer},
            device_id_type=MESH,
        )

    def note_from(step):
        peer = lax.rem(me + step, ranks)
        return pltpu.make_async_remote_copy(
            src_ref=note_out.at[peer],
            dst_ref=note_in.at[peer],
            send_sem=note_send.at[peer],
            recv_sem=note_recv.at[peer],
            device_id={"ep": peer},
            device_id_type=MESH,
        )

    def send_note(step, carry):
        peer = peer_of(step)

        @pl.when(peer != me)
        def _():
            note_to(peer).start()

        return carry

    lax.fori_loop(0, ranks, send_note, 0)

    def produce(b, tiles):
        for j in tiles:
            if b == 0:
                columns[j].wait()
            produced[b, :, j * TILE : (j + 1) * TILE] = jnp.dot(
                hidden[b], weight[j], preferred_element_type=jnp.float32
            ).astype(jnp.bfloat16)

    tiles = width // TILE
    spans = (width, width // 2)
    loads[2].wait()
    produce(0, range(tiles))
    produce(1, range(tiles))

    def take_note(step, carry):
        note_from(step).wait_recv()
        return carry

    lax.fori_loop(1, ranks, take_note, 0)

    flags = note_in[...].reshape(ranks, 128)
    upper = lax.broadcasted_iota(jnp.int32, (128, 128), 0)
    lower = lax.broadcasted_iota(jnp.int32, (128, 128), 1)
    alike = (upper >= both) & (upper < 2 * both) & (lower >= both) & (lower < 2 * both)
    alike = alike & (upper // rows == lower // rows)
    ones = jnp.where(alike, 1.0, 0.0).astype(jnp.bfloat16)
    ahead = jnp.where(alike & (upper < lower), 1.0, 0.0).astype(jnp.bfloat16)
    packed = flags.astype(jnp.bfloat16)
    within = jnp.dot(packed, ahead, preferred_element_type=jnp.float32)
    counts = jnp.dot(packed, ones, preferred_element_type=jnp.float32).astype(jnp.bfloat16)
    earlier = lax.broadcasted_iota(jnp.int32, (ranks, ranks), 1) < lax.broadcasted_iota(
        jnp.int32, (ranks, ranks), 0
    )
    before = jnp.dot(
        jnp.where(earlier, 1.0, 0.0).astype(jnp.bfloat16), counts, preferred_element_type=jnp.float32
    )
    slot_of[...] = jnp.where(flags > 0.5, within + before, -1.0).reshape(ranks, 1, 128)

    lane = lax.broadcasted_iota(jnp.int32, (rows, 128), 1)
    row = lax.broadcasted_iota(jnp.int32, (rows, 128), 0)
    slot = lax.broadcasted_iota(jnp.int32, (8 * rows, slots), 1).astype(jnp.float32)

    def core_copy(i, b):
        return pltpu.make_async_remote_copy(
            src_ref=core_out.at[i, b], dst_ref=core_in.at[i, b],
            send_sem=core_send.at[i, b], recv_sem=core_recv.at[i, b],
            device_id={"ep": sibling}, device_id_type=MESH,
        )

    def x_copy(i, b):
        cut = pl.ds(0, spans[b])
        return pltpu.make_async_remote_copy(
            src_ref=x_out.at[i, b, :, cut], dst_ref=x_in.at[i, b, :, cut],
            send_sem=x_send.at[i, b], recv_sem=x_recv.at[i, b],
            device_id={"ep": beside}, device_id_type=MESH,
        )

    def z_copy(i, b):
        cut = pl.ds(0, spans[b])
        return pltpu.make_async_remote_copy(
            src_ref=z_out.at[i, b, :, cut], dst_ref=z_in.at[i, b, :, cut],
            send_sem=z_send.at[i, b], recv_sem=z_recv.at[i, b],
            device_id={"ep": far if i == 1 else near}, device_id_type=MESH,
        )

    def spread(parts, b):
        factor, place = [], []
        for i in parts:
            plane = 2 * lax.rem(high + 1 - i // 2, 2) + lax.rem(low + 1 - i % 2, 2)
            for other_core in (1, 0):
                for other_x in (1, 0):
                    c = lax.rem(core + other_core, 2)
                    at_x = lax.rem(x + other_x, 2)
                    owner = plane * 4 + at_x * 2 + c
                    note, spot = note_in[owner], slot_of[owner]
                    factor.append(
                        jnp.sum(jnp.where(lane == row + b * rows, note, 0.0), axis=1, keepdims=True)
                    )
                    place.append(
                        jnp.sum(
                            jnp.where(lane == row + (both + b * rows), spot, 0.0),
                            axis=1, keepdims=True,
                        )
                    )
        scale = jnp.concatenate(factor, axis=0)
        pick = jnp.where(jnp.concatenate(place, axis=0) == slot, 1.0, 0.0).astype(jnp.bfloat16)
        for j in range(tiles):
            cut = slice(j * TILE, (j + 1) * TILE)
            part = scale * jnp.dot(pick, produced[b, :, cut], preferred_element_type=jnp.float32)
            for step, i in enumerate(parts):
                top = 4 * rows * step
                core_out[i, b, :, cut] = part[top : top + 2 * rows].astype(jnp.bfloat16)
                core_kept[i, b, :, cut] = part[top + 2 * rows : top + 4 * rows]
        for i in parts:
            core_copy(i, b).start()

    def near_copy(k):
        return pltpu.make_async_remote_copy(
            src_ref=near_out.at[k], dst_ref=near_in.at[k],
            send_sem=near_send.at[k], recv_sem=near_recv.at[k],
            device_id={"ep": near}, device_id_type=MESH,
        )

    def side_copy(k):
        return pltpu.make_async_remote_copy(
            src_ref=side_out.at[k], dst_ref=side_in.at[k],
            send_sem=side_send.at[k], recv_sem=side_recv.at[k],
            device_id={"ep": beside}, device_id_type=MESH,
        )

    def far_copy():
        return pltpu.make_async_remote_copy(
            src_ref=far_out.at[0], dst_ref=far_in.at[0],
            send_sem=far_send.at[0], recv_sem=far_recv.at[0],
            device_id={"ep": far}, device_id_type=MESH,
        )

    def over_cores(i, b):
        core_copy(i, b).wait_recv()
        n = spans[b]
        total = core_kept[i, b, :, :n] + core_in[i, b, :, :n].astype(jnp.float32)
        x_out[i, b, :, :n] = total[:rows].astype(jnp.bfloat16)
        x_kept[i, b, :, :n] = total[rows:]
        x_copy(i, b).start()
        if b == 1:
            total = core_kept[i, b, :, n:] + core_in[i, b, :, n:].astype(jnp.float32)
            if i % 2 == 0:
                near_out[i // 2] = total.astype(jnp.bfloat16)
                near_copy(i // 2).start()
            else:
                near_kept[i // 2] = total

    def over_near(k):
        near_copy(k).wait_recv()
        total = near_kept[k] + near_in[k].astype(jnp.float32)
        side_out[k] = total[:rows].astype(jnp.bfloat16)
        side_kept[k] = total[rows:]
        side_copy(k).start()

    def over_side(k):
        side_copy(k).wait_recv()
        total = side_kept[k] + side_in[k].astype(jnp.float32)
        if k == 0:
            far_out[0] = total.astype(jnp.bfloat16)
            far_copy().start()
        else:
            n = spans[1]
            total = total + residual[1, :, n:].astype(jnp.float32)
            far_copy().wait_recv()
            mixed_ref[1, :, n:] = (total + far_in[0].astype(jnp.float32)).astype(jnp.bfloat16)

    def over_x(i, b):
        n = spans[b]
        x_copy(i, b).wait_recv()
        total = x_kept[i, b, :, :n] + x_in[i, b, :, :n].astype(jnp.float32)
        if i == 1:
            z_copy(0, b).wait_recv()
            total = total + z_in[0, b, :, :n].astype(jnp.float32)
        if i < 3:
            z_out[i, b, :, :n] = total.astype(jnp.bfloat16)
            z_copy(i, b).start()
        else:
            total = total + residual[b, :, :n].astype(jnp.float32)
            z_copy(2, b).wait_recv()
            total = total + z_in[2, b, :, :n].astype(jnp.float32)
            z_copy(1, b).wait_recv()
            mixed_ref[b, :, :n] = (total + z_in[1, b, :, :n].astype(jnp.float32)).astype(
                jnp.bfloat16
            )

    spread((0, 1), 0)
    spread((0, 1), 1)
    over_cores(0, 0)
    over_cores(0, 1)
    over_cores(1, 0)
    over_cores(1, 1)
    spread((2, 3), 0)
    over_cores(2, 0)
    over_x(0, 0)
    over_cores(3, 0)
    spread((2, 3), 1)
    over_near(0)
    over_cores(2, 1)
    over_cores(3, 1)
    over_x(0, 1)
    over_x(1, 0)
    over_x(1, 1)
    over_near(1)
    over_x(2, 0)
    over_side(0)
    over_x(2, 1)
    residual_load.wait()
    over_x(3, 0)
    over_x(3, 1)
    over_side(1)

    for b in range(batches):
        for i in range(4):
            core_copy(i, b).wait_send()
            x_copy(i, b).wait_send()
            if i < 3:
                z_copy(i, b).wait_send()
    for k in range(2):
        near_copy(k).wait_send()
        side_copy(k).wait_send()
    far_copy().wait_send()

    def note_left(step, carry):
        note_to(lax.rem(me + step, ranks)).wait_send()
        return carry

    lax.fori_loop(1, ranks, note_left, 0)


def dense_shards(ranks, hidden, down_weight, routes, route_weight, residual):
    batches, rows, chosen = routes.shape
    slots, depth = hidden.shape[2:]
    width = down_weight.shape[2]
    both = batches * rows
    bf16, f32 = jnp.bfloat16, jnp.float32
    sizes = (ranks, batches, rows, chosen, slots, width)
    parts = 4
    return pl.pallas_call(
        functools.partial(dense_kernel, sizes),
        out_shape=jax.ShapeDtypeStruct((batches, rows, width), bf16),
        in_specs=[pl.BlockSpec(memory_space=pl.ANY)] * 5,
        out_specs=pl.BlockSpec(memory_space=pltpu.VMEM),
        scratch_shapes=[
            pltpu.VMEM((batches, slots, depth), bf16),
            pltpu.VMEM((width // TILE, depth, TILE), bf16),
            pltpu.VMEM((batches, chosen, rows), jnp.int32),
            pltpu.VMEM((batches, chosen, rows), f32),
            pltpu.VMEM((batches, rows, width), bf16),
            pltpu.VMEM((batches, slots, width), bf16),
            pltpu.VMEM((ranks, 1, 128), f32),
            pltpu.VMEM((ranks, 1, 128), f32),
            pltpu.VMEM((ranks, 1, 128), f32),
            pltpu.VMEM((parts, batches, 2 * rows, width), bf16),
            pltpu.VMEM((parts, batches, 2 * rows, width), bf16),
            pltpu.VMEM((parts, batches, 2 * rows, width), f32),
            pltpu.VMEM((parts, batches, rows, width), bf16),
            pltpu.VMEM((parts, batches, rows, width), bf16),
            pltpu.VMEM((parts, batches, rows, width), f32),
            pltpu.VMEM((3, batches, rows, width), bf16),
            pltpu.VMEM((3, batches, rows, width), bf16),
            pltpu.VMEM((2, 2 * rows, width // 2), bf16),
            pltpu.VMEM((2, 2 * rows, width // 2), bf16),
            pltpu.VMEM((2, 2 * rows, width // 2), f32),
            pltpu.VMEM((2, rows, width // 2), bf16),
            pltpu.VMEM((2, rows, width // 2), bf16),
            pltpu.VMEM((2, rows, width // 2), f32),
            pltpu.VMEM((1, rows, width // 2), bf16),
            pltpu.VMEM((1, rows, width // 2), bf16),
            pltpu.SemaphoreType.DMA((4,)),
            pltpu.SemaphoreType.DMA((width // TILE,)),
            pltpu.SemaphoreType.DMA((ranks,)),
            pltpu.SemaphoreType.DMA((ranks,)),
            pltpu.SemaphoreType.DMA((parts, batches)),
            pltpu.SemaphoreType.DMA((parts, batches)),
            pltpu.SemaphoreType.DMA((parts, batches)),
            pltpu.SemaphoreType.DMA((parts, batches)),
            pltpu.SemaphoreType.DMA((3, batches)),
            pltpu.SemaphoreType.DMA((3, batches)),
            pltpu.SemaphoreType.DMA((2,)),
            pltpu.SemaphoreType.DMA((2,)),
            pltpu.SemaphoreType.DMA((2,)),
            pltpu.SemaphoreType.DMA((2,)),
            pltpu.SemaphoreType.DMA((1,)),
            pltpu.SemaphoreType.DMA((1,)),
        ],
        compiler_params=pltpu.CompilerParams(
            collective_id=0, has_side_effects=True, vmem_limit_bytes=48 * 1024 * 1024
        ),
    )(
        *[
            pltpu.with_memory_space_constraint(operand, pltpu.HBM)
            for operand in (
                hidden.reshape(batches, slots, depth),
                down_weight.reshape(depth, width),
                jnp.swapaxes(routes, 1, 2),
                jnp.swapaxes(route_weight, 1, 2),
                residual,
            )
        ]
    )


def solution(mesh):
    ranks = mesh.shape["ep"]
    in_specs = (
        P("dp", "ep", None, None),
        P("ep", None, None),
        P("dp", "ep", None),
        P("dp", "ep", None),
        P("dp", "ep", None),
    )
    out_specs = P("dp", "ep", None)

    def run(hidden, down_weight, routes, route_weight, residual):
        rows = routes.shape[1] // ranks
        batches = routes.shape[0] // mesh.shape["dp"]
        dense = ranks == 16 and rows % 16 == 0 and routes.shape[1] <= hidden.shape[2]
        dense = dense and batches == 2 and 2 * batches * rows <= 128
        body = functools.partial(dense_shards, ranks) if dense else shards
        return jax.shard_map(
            body, mesh=mesh, in_specs=in_specs, out_specs=out_specs, check_vma=False
        )(hidden, down_weight, routes, route_weight, residual)

    return run
```

```python
import functools
import math

import jax
import jax.numpy as jnp
from jax import lax
from jax.experimental import pallas as pl
from jax.experimental.pallas import tpu as pltpu
from jax.sharding import PartitionSpec as P


def shards(hidden, down_weight, routes, route_weight, residual):
    ranks_total = lax.axis_size("ep")
    batch_count = routes.shape[0]
    row_count = routes.shape[1]
    choose_count = routes.shape[2]
    slot_count = hidden.shape[2]
    per_peer = slot_count // ranks_total
    model_width = down_weight.shape[2]
    matrix = down_weight[0]
    labels = jnp.arange(ranks_total, dtype=jnp.int32)
    picked = jnp.sum((routes[:, :, :, None] == labels).astype(jnp.int32), axis=2, dtype=jnp.int32)
    rank_in_block = jnp.take_along_axis(
        jnp.cumsum(picked, axis=1, dtype=jnp.int32) - picked, routes, axis=2
    )
    loads_out = jnp.transpose(jnp.sum(picked, axis=1, dtype=jnp.int32))
    loads_in = lax.all_to_all(loads_out, "ep", split_axis=0, concat_axis=0, tiled=True)
    arriving = jnp.transpose(loads_in)
    offsets = jnp.cumsum(arriving, axis=1, dtype=jnp.int32) - arriving
    totals = jnp.sum(arriving, axis=1, dtype=jnp.int32)
    results = []
    for batch_index in range(batch_count):
        packed = hidden[batch_index, 0]
        block_size = math.gcd(slot_count, 128)

        def add_block(block_index, produced_in):
            begin_at = block_index * block_size
            segment = lax.dynamic_slice_in_dim(packed, begin_at, block_size, 0)
            product = jnp.dot(segment, matrix, preferred_element_type=jnp.float32).astype(
                jnp.bfloat16
            )
            return lax.dynamic_update_slice_in_dim(produced_in, product, begin_at, 0)

        block_count = (totals[batch_index] + block_size - 1) // block_size
        expert_produced = lax.fori_loop(
            0, block_count, add_block, jnp.zeros((slot_count, model_width), jnp.bfloat16)
        )
        selector = offsets[batch_index][:, None] + jnp.arange(per_peer, dtype=jnp.int32)[None, :]
        selector = jnp.minimum(selector, slot_count - 1)
        sending = jnp.take(expert_produced, selector.reshape(-1), axis=0).reshape(
            ranks_total, per_peer, model_width
        )
        arrived = lax.all_to_all(sending, "ep", split_axis=0, concat_axis=0, tiled=True)
        flattened = arrived.reshape(ranks_total * per_peer, model_width)
        location = routes[batch_index] * per_peer + rank_in_block[batch_index]
        gathered = jnp.take(flattened, location.reshape(-1), axis=0).reshape(
            row_count, choose_count, model_width
        )
        weighted = jnp.sum(
            route_weight[batch_index][:, :, None] * gathered.astype(jnp.float32), axis=1
        )
        results.append((residual[batch_index].astype(jnp.float32) + weighted).astype(jnp.bfloat16))
    return jnp.stack(results, axis=0)


MESH = pl.DeviceIdType.MESH
TILE = 512


def dense_kernel(
    sizes, hidden_hbm, weight_hbm, routes_hbm, shares_hbm, residual_hbm, mixed_ref,
    hidden, weight, routes, shares, residual, produced,
    note_out, note_in, slot_of,
    core_out, core_in, core_kept, x_out, x_in, x_kept, z_out, z_in, near_out, near_in, near_kept,
    load_sem, column_sem, note_send, note_recv, core_send, core_recv, x_send, x_recv, z_send, z_recv,
    near_send, near_recv,
):
    ranks, batches, rows, chosen, slots, width = sizes
    both = batches * rows
    me = lax.axis_index("ep")
    core, x, z = lax.rem(me, 2), lax.rem(me // 2, 2), me // 4
    low, high = lax.rem(z, 2), z // 2
    sibling = me + 1 - 2 * core
    beside = me + 2 - 4 * x
    near = me + 4 - 8 * low
    far = me + 8 - 16 * high

    barrier = pltpu.get_barrier_semaphore()

    turn = 2 * (me // (ranks // 2)) - 1

    def peer_of(step):
        return lax.rem(2 * ranks - 1 - me + turn * step, ranks)

    def greet(step, carry):
        peer = peer_of(step)

        @pl.when(peer != me)
        def _():
            pl.semaphore_signal(barrier, inc=1, device_id={"ep": peer}, device_id_type=MESH)

        return carry

    lax.fori_loop(0, ranks, greet, 0)

    loads = [
        pltpu.make_async_copy(routes_hbm, routes, load_sem.at[0]),
        pltpu.make_async_copy(shares_hbm, shares, load_sem.at[1]),
        pltpu.make_async_copy(hidden_hbm, hidden, load_sem.at[2]),
    ]
    columns = [
        pltpu.make_async_copy(
            weight_hbm.at[:, pl.ds(j * TILE, TILE)], weight.at[j], column_sem.at[j]
        )
        for j in range(width // TILE)
    ]
    residual_load = pltpu.make_async_copy(residual_hbm, residual, load_sem.at[3])
    for copy in loads + columns + [residual_load]:
        copy.start()

    loads[0].wait()
    loads[1].wait()
    given, named = [], []
    expert = lax.broadcasted_iota(jnp.int32, (ranks, chosen, rows), 0)
    for b in range(batches):
        hit = routes[b][None] == expert
        given.append(jnp.sum(jnp.where(hit, shares[b][None], 0.0), axis=1))
        named.append(jnp.sum(jnp.where(hit, 1.0, 0.0), axis=1))
    notes = jnp.concatenate(
        given + named + [jnp.zeros((ranks, 128 - 2 * both), jnp.float32)], axis=1
    )
    note_out[...] = notes.reshape(ranks, 1, 128)
    note_in[pl.ds(me, 1)] = note_out[pl.ds(me, 1)]

    pl.semaphore_wait(barrier, ranks - 1)

    def note_to(peer):
        return pltpu.make_async_remote_copy(
            src_ref=note_out.at[peer],
            dst_ref=note_in.at[me],
            send_sem=note_send.at[peer],
            recv_sem=note_recv.at[me],
            device_id={"ep": peer},
            device_id_type=MESH,
        )

    def note_from(step):
        peer = lax.rem(me + step, ranks)
        return pltpu.make_async_remote_copy(
            src_ref=note_out.at[peer],
            dst_ref=note_in.at[peer],
            send_sem=note_send.at[peer],
            recv_sem=note_recv.at[peer],
            device_id={"ep": peer},
            device_id_type=MESH,
        )

    def send_note(step, carry):
        peer = peer_of(step)

        @pl.when(peer != me)
        def _():
            note_to(peer).start()

        return carry

    lax.fori_loop(0, ranks, send_note, 0)

    def produce(b, tiles):
        for j in tiles:
            if b == 0:
                columns[j].wait()
            produced[b, :, j * TILE : (j + 1) * TILE] = jnp.dot(
                hidden[b], weight[j], preferred_element_type=jnp.float32
            ).astype(jnp.bfloat16)

    tiles = width // TILE
    loads[2].wait()
    produce(0, range(tiles))
    produce(1, range(tiles))

    def take_note(step, carry):
        note_from(step).wait_recv()
        return carry

    lax.fori_loop(1, ranks, take_note, 0)

    flags = note_in[...].reshape(ranks, 128)
    upper = lax.broadcasted_iota(jnp.int32, (128, 128), 0)
    lower = lax.broadcasted_iota(jnp.int32, (128, 128), 1)
    alike = (upper >= both) & (upper < 2 * both) & (lower >= both) & (lower < 2 * both)
    alike = alike & (upper // rows == lower // rows)
    ones = jnp.where(alike, 1.0, 0.0).astype(jnp.bfloat16)
    ahead = jnp.where(alike & (upper < lower), 1.0, 0.0).astype(jnp.bfloat16)
    packed = flags.astype(jnp.bfloat16)
    within = jnp.dot(packed, ahead, preferred_element_type=jnp.float32)
    counts = jnp.dot(packed, ones, preferred_element_type=jnp.float32).astype(jnp.bfloat16)
    earlier = lax.broadcasted_iota(jnp.int32, (ranks, ranks), 1) < lax.broadcasted_iota(
        jnp.int32, (ranks, ranks), 0
    )
    before = jnp.dot(
        jnp.where(earlier, 1.0, 0.0).astype(jnp.bfloat16), counts, preferred_element_type=jnp.float32
    )
    slot_of[...] = jnp.where(flags > 0.5, within + before, -1.0).reshape(ranks, 1, 128)

    lane = lax.broadcasted_iota(jnp.int32, (rows, 128), 1)
    row = lax.broadcasted_iota(jnp.int32, (rows, 128), 0)
    slot = lax.broadcasted_iota(jnp.int32, (8 * rows, slots), 1).astype(jnp.float32)

    def core_copy(i, b):
        return pltpu.make_async_remote_copy(
            src_ref=core_out.at[i, b], dst_ref=core_in.at[i, b],
            send_sem=core_send.at[i, b], recv_sem=core_recv.at[i, b],
            device_id={"ep": sibling}, device_id_type=MESH,
        )

    def x_copy(i, b):
        return pltpu.make_async_remote_copy(
            src_ref=x_out.at[i, b], dst_ref=x_in.at[i, b],
            send_sem=x_send.at[i, b], recv_sem=x_recv.at[i, b],
            device_id={"ep": beside}, device_id_type=MESH,
        )

    def z_copy(i, b):
        return pltpu.make_async_remote_copy(
            src_ref=z_out.at[i, b], dst_ref=z_in.at[i, b],
            send_sem=z_send.at[i, b], recv_sem=z_recv.at[i, b],
            device_id={"ep": far if i == 1 else near}, device_id_type=MESH,
        )

    def spread(parts, b):
        factor, place = [], []
        for i in parts:
            plane = 2 * lax.rem(high + 1 - i // 2, 2) + lax.rem(low + 1 - i % 2, 2)
            for other_core in (1, 0):
                for other_x in (1, 0):
                    c = lax.rem(core + other_core, 2)
                    at_x = lax.rem(x + other_x, 2)
                    owner = plane * 4 + at_x * 2 + c
                    note, spot = note_in[owner], slot_of[owner]
                    factor.append(
                        jnp.sum(jnp.where(lane == row + b * rows, note, 0.0), axis=1, keepdims=True)
                    )
                    place.append(
                        jnp.sum(
                            jnp.where(lane == row + (both + b * rows), spot, 0.0),
                            axis=1, keepdims=True,
                        )
                    )
        scale = jnp.concatenate(factor, axis=0)
        pick = jnp.where(jnp.concatenate(place, axis=0) == slot, 1.0, 0.0).astype(jnp.bfloat16)
        for j in range(tiles):
            cut = slice(j * TILE, (j + 1) * TILE)
            part = scale * jnp.dot(pick, produced[b, :, cut], preferred_element_type=jnp.float32)
            for step, i in enumerate(parts):
                top = 4 * rows * step
                core_out[i, b, :, cut] = part[top : top + 2 * rows].astype(jnp.bfloat16)
                core_kept[i, b, :, cut] = part[top + 2 * rows : top + 4 * rows]
        for i in parts:
            core_copy(i, b).start()

    def near_copy(k):
        return pltpu.make_async_remote_copy(
            src_ref=near_out.at[k], dst_ref=near_in.at[k],
            send_sem=near_send.at[k], recv_sem=near_recv.at[k],
            device_id={"ep": near}, device_id_type=MESH,
        )

    def over_cores(i, b):
        core_copy(i, b).wait_recv()
        total = core_kept[i, b] + core_in[i, b].astype(jnp.float32)
        if b == 0:
            x_out[i, b] = total[:rows].astype(jnp.bfloat16)
            x_kept[i, b] = total[rows:]
            x_copy(i, b).start()
        elif i % 2 == 0:
            near_out[i // 2] = total.astype(jnp.bfloat16)
            near_copy(i // 2).start()
        else:
            near_kept[i // 2] = total

    def over_near(i):
        near_copy(i // 2).wait_recv()
        total = near_kept[i // 2] + near_in[i // 2].astype(jnp.float32)
        x_out[i, 1] = total[:rows].astype(jnp.bfloat16)
        x_kept[i, 1] = total[rows:]
        x_copy(i, 1).start()

    def over_x(i, b):
        x_copy(i, b).wait_recv()
        total = x_kept[i, b] + x_in[i, b].astype(jnp.float32)
        if i == 1 and b == 0:
            z_copy(0, b).wait_recv()
            total = total + z_in[0, b].astype(jnp.float32)
        if i < 3:
            z_out[i, b] = total.astype(jnp.bfloat16)
            z_copy(i, b).start()
        else:
            total = total + residual[b].astype(jnp.float32)
            if b == 0:
                z_copy(2, b).wait_recv()
                total = total + z_in[2, b].astype(jnp.float32)
            z_copy(1, b).wait_recv()
            mixed_ref[b] = (total + z_in[1, b].astype(jnp.float32)).astype(jnp.bfloat16)

    spread((0, 1), 0)
    spread((0, 1), 1)
    over_cores(0, 0)
    over_cores(0, 1)
    over_cores(1, 0)
    over_cores(1, 1)
    spread((2, 3), 0)
    over_cores(2, 0)
    over_x(0, 0)
    over_cores(3, 0)
    spread((2, 3), 1)
    over_near(1)
    over_cores(2, 1)
    over_cores(3, 1)
    def note_left(step, carry):
        note_to(lax.rem(me + step, ranks)).wait_send()
        return carry

    over_x(1, 0)
    lax.fori_loop(1, ranks, note_left, 0)
    over_x(2, 0)
    for i in range(4):
        for b in range(batches):
            core_copy(i, b).wait_send()
    over_x(1, 1)
    over_near(3)
    residual_load.wait()
    for i in range(4):
        x_copy(i, 0).wait_send()
    for k in range(2):
        near_copy(k).wait_send()
    over_x(3, 0)
    z_copy(0, 0).wait_send()
    z_copy(2, 0).wait_send()
    x_copy(1, 1).wait_send()
    over_x(3, 1)
    x_copy(3, 1).wait_send()
    z_copy(1, 0).wait_send()
    z_copy(1, 1).wait_send()


def dense_shards(ranks, hidden, down_weight, routes, route_weight, residual):
    batches, rows, chosen = routes.shape
    slots, depth = hidden.shape[2:]
    width = down_weight.shape[2]
    both = batches * rows
    bf16, f32 = jnp.bfloat16, jnp.float32
    sizes = (ranks, batches, rows, chosen, slots, width)
    parts = 4
    return pl.pallas_call(
        functools.partial(dense_kernel, sizes),
        out_shape=jax.ShapeDtypeStruct((batches, rows, width), bf16),
        in_specs=[pl.BlockSpec(memory_space=pl.ANY)] * 5,
        out_specs=pl.BlockSpec(memory_space=pltpu.VMEM),
        scratch_shapes=[
            pltpu.VMEM((batches, slots, depth), bf16),
            pltpu.VMEM((width // TILE, depth, TILE), bf16),
            pltpu.VMEM((batches, chosen, rows), jnp.int32),
            pltpu.VMEM((batches, chosen, rows), f32),
            pltpu.VMEM((batches, rows, width), bf16),
            pltpu.VMEM((batches, slots, width), bf16),
            pltpu.VMEM((ranks, 1, 128), f32),
            pltpu.VMEM((ranks, 1, 128), f32),
            pltpu.VMEM((ranks, 1, 128), f32),
            pltpu.VMEM((parts, batches, 2 * rows, width), bf16),
            pltpu.VMEM((parts, batches, 2 * rows, width), bf16),
            pltpu.VMEM((parts, batches, 2 * rows, width), f32),
            pltpu.VMEM((parts, batches, rows, width), bf16),
            pltpu.VMEM((parts, batches, rows, width), bf16),
            pltpu.VMEM((parts, batches, rows, width), f32),
            pltpu.VMEM((3, batches, rows, width), bf16),
            pltpu.VMEM((3, batches, rows, width), bf16),
            pltpu.VMEM((2, 2 * rows, width), bf16),
            pltpu.VMEM((2, 2 * rows, width), bf16),
            pltpu.VMEM((2, 2 * rows, width), f32),
            pltpu.SemaphoreType.DMA((4,)),
            pltpu.SemaphoreType.DMA((width // TILE,)),
            pltpu.SemaphoreType.DMA((ranks,)),
            pltpu.SemaphoreType.DMA((ranks,)),
            pltpu.SemaphoreType.DMA((parts, batches)),
            pltpu.SemaphoreType.DMA((parts, batches)),
            pltpu.SemaphoreType.DMA((parts, batches)),
            pltpu.SemaphoreType.DMA((parts, batches)),
            pltpu.SemaphoreType.DMA((3, batches)),
            pltpu.SemaphoreType.DMA((3, batches)),
            pltpu.SemaphoreType.DMA((2,)),
            pltpu.SemaphoreType.DMA((2,)),
        ],
        compiler_params=pltpu.CompilerParams(
            collective_id=0, has_side_effects=True, vmem_limit_bytes=48 * 1024 * 1024
        ),
    )(
        *[
            pltpu.with_memory_space_constraint(operand, pltpu.HBM)
            for operand in (
                hidden.reshape(batches, slots, depth),
                down_weight.reshape(depth, width),
                jnp.swapaxes(routes, 1, 2),
                jnp.swapaxes(route_weight, 1, 2),
                residual,
            )
        ]
    )


def solution(mesh):
    ranks = mesh.shape["ep"]
    in_specs = (
        P("dp", "ep", None, None),
        P("ep", None, None),
        P("dp", "ep", None),
        P("dp", "ep", None),
        P("dp", "ep", None),
    )
    out_specs = P("dp", "ep", None)

    def run(hidden, down_weight, routes, route_weight, residual):
        rows = routes.shape[1] // ranks
        batches = routes.shape[0] // mesh.shape["dp"]
        dense = ranks == 16 and rows % 16 == 0 and routes.shape[1] <= hidden.shape[2]
        dense = dense and batches == 2 and 2 * batches * rows <= 128
        body = functools.partial(dense_shards, ranks) if dense else shards
        return jax.shard_map(
            body, mesh=mesh, in_specs=in_specs, out_specs=out_specs, check_vma=False
        )(hidden, down_weight, routes, route_weight, residual)

    return run
```

```python
import functools
import math

import jax
import jax.numpy as jnp
from jax import lax
from jax.experimental import pallas as pl
from jax.experimental.pallas import tpu as pltpu
from jax.sharding import PartitionSpec as P


def shards(hidden, down_weight, routes, route_weight, residual):
    ranks_total = lax.axis_size("ep")
    batch_count = routes.shape[0]
    row_count = routes.shape[1]
    choose_count = routes.shape[2]
    slot_count = hidden.shape[2]
    per_peer = slot_count // ranks_total
    model_width = down_weight.shape[2]
    matrix = down_weight[0]
    labels = jnp.arange(ranks_total, dtype=jnp.int32)
    picked = jnp.sum((routes[:, :, :, None] == labels).astype(jnp.int32), axis=2, dtype=jnp.int32)
    rank_in_block = jnp.take_along_axis(
        jnp.cumsum(picked, axis=1, dtype=jnp.int32) - picked, routes, axis=2
    )
    loads_out = jnp.transpose(jnp.sum(picked, axis=1, dtype=jnp.int32))
    loads_in = lax.all_to_all(loads_out, "ep", split_axis=0, concat_axis=0, tiled=True)
    arriving = jnp.transpose(loads_in)
    offsets = jnp.cumsum(arriving, axis=1, dtype=jnp.int32) - arriving
    totals = jnp.sum(arriving, axis=1, dtype=jnp.int32)
    results = []
    for batch_index in range(batch_count):
        packed = hidden[batch_index, 0]
        block_size = math.gcd(slot_count, 128)

        def add_block(block_index, produced_in):
            begin_at = block_index * block_size
            segment = lax.dynamic_slice_in_dim(packed, begin_at, block_size, 0)
            product = jnp.dot(segment, matrix, preferred_element_type=jnp.float32).astype(
                jnp.bfloat16
            )
            return lax.dynamic_update_slice_in_dim(produced_in, product, begin_at, 0)

        block_count = (totals[batch_index] + block_size - 1) // block_size
        expert_produced = lax.fori_loop(
            0, block_count, add_block, jnp.zeros((slot_count, model_width), jnp.bfloat16)
        )
        selector = offsets[batch_index][:, None] + jnp.arange(per_peer, dtype=jnp.int32)[None, :]
        selector = jnp.minimum(selector, slot_count - 1)
        sending = jnp.take(expert_produced, selector.reshape(-1), axis=0).reshape(
            ranks_total, per_peer, model_width
        )
        arrived = lax.all_to_all(sending, "ep", split_axis=0, concat_axis=0, tiled=True)
        flattened = arrived.reshape(ranks_total * per_peer, model_width)
        location = routes[batch_index] * per_peer + rank_in_block[batch_index]
        gathered = jnp.take(flattened, location.reshape(-1), axis=0).reshape(
            row_count, choose_count, model_width
        )
        weighted = jnp.sum(
            route_weight[batch_index][:, :, None] * gathered.astype(jnp.float32), axis=1
        )
        results.append((residual[batch_index].astype(jnp.float32) + weighted).astype(jnp.bfloat16))
    return jnp.stack(results, axis=0)


MESH = pl.DeviceIdType.MESH
TILE = 512


def dense_kernel(
    sizes, hidden_hbm, weight_hbm, routes_hbm, shares_hbm, residual_hbm, mixed_ref,
    hidden, weight, routes, shares, residual, produced,
    note_out, note_in, slot_of,
    core_out, core_in, core_kept, x_out, x_in, x_kept, z_out, z_in, near_out, near_in, near_kept,
    load_sem, column_sem, note_send, note_recv, core_send, core_recv, x_send, x_recv, z_send, z_recv,
    near_send, near_recv,
):
    ranks, batches, rows, chosen, slots, width = sizes
    both = batches * rows
    me = lax.axis_index("ep")
    core, x, z = lax.rem(me, 2), lax.rem(me // 2, 2), me // 4
    low, high = lax.rem(z, 2), z // 2
    sibling = me + 1 - 2 * core
    beside = me + 2 - 4 * x
    near = me + 4 - 8 * low
    far = me + 8 - 16 * high

    barrier = pltpu.get_barrier_semaphore()

    turn = 2 * (me // (ranks // 2)) - 1

    def peer_of(step):
        return lax.rem(2 * ranks - 1 - me + turn * step, ranks)

    def greet(step, carry):
        peer = peer_of(step)

        @pl.when(peer != me)
        def _():
            pl.semaphore_signal(barrier, inc=1, device_id={"ep": peer}, device_id_type=MESH)

        return carry

    loads = [
        pltpu.make_async_copy(routes_hbm, routes, load_sem.at[0]),
        pltpu.make_async_copy(shares_hbm, shares, load_sem.at[1]),
        pltpu.make_async_copy(hidden_hbm, hidden, load_sem.at[2]),
    ]
    columns = [
        pltpu.make_async_copy(
            weight_hbm.at[:, pl.ds(j * TILE, TILE)], weight.at[j], column_sem.at[j]
        )
        for j in range(width // TILE)
    ]
    residual_load = pltpu.make_async_copy(residual_hbm, residual, load_sem.at[3])
    loads[0].start()
    loads[1].start()
    lax.fori_loop(0, ranks, greet, 0)
    for copy in loads[2:] + columns + [residual_load]:
        copy.start()

    loads[0].wait()
    loads[1].wait()
    given, named = [], []
    expert = lax.broadcasted_iota(jnp.int32, (ranks, chosen, rows), 0)
    for b in range(batches):
        hit = routes[b][None] == expert
        given.append(jnp.sum(jnp.where(hit, shares[b][None], 0.0), axis=1))
        named.append(jnp.sum(jnp.where(hit, 1.0, 0.0), axis=1))
    notes = jnp.concatenate(
        given + named + [jnp.zeros((ranks, 128 - 2 * both), jnp.float32)], axis=1
    )
    note_out[...] = notes.reshape(ranks, 1, 128)
    note_in[pl.ds(me, 1)] = note_out[pl.ds(me, 1)]

    pl.semaphore_wait(barrier, ranks - 1)

    def note_to(peer):
        return pltpu.make_async_remote_copy(
            src_ref=note_out.at[peer],
            dst_ref=note_in.at[me],
            send_sem=note_send.at[peer],
            recv_sem=note_recv.at[me],
            device_id={"ep": peer},
            device_id_type=MESH,
        )

    def note_from(step):
        peer = lax.rem(me + step, ranks)
        return pltpu.make_async_remote_copy(
            src_ref=note_out.at[peer],
            dst_ref=note_in.at[peer],
            send_sem=note_send.at[peer],
            recv_sem=note_recv.at[peer],
            device_id={"ep": peer},
            device_id_type=MESH,
        )

    def send_note(step, carry):
        peer = peer_of(step)

        @pl.when(peer != me)
        def _():
            note_to(peer).start()

        return carry

    lax.fori_loop(0, ranks, send_note, 0)

    def produce(b, tiles):
        for j in tiles:
            if b == 0:
                columns[j].wait()
            produced[b, :, j * TILE : (j + 1) * TILE] = jnp.dot(
                hidden[b], weight[j], preferred_element_type=jnp.float32
            ).astype(jnp.bfloat16)

    tiles = width // TILE
    loads[2].wait()
    produce(0, range(tiles))
    produce(1, range(tiles))

    def take_note(step, carry):
        note_from(step).wait_recv()
        return carry

    lax.fori_loop(1, ranks, take_note, 0)

    flags = note_in[...].reshape(ranks, 128)
    upper = lax.broadcasted_iota(jnp.int32, (128, 128), 0)
    lower = lax.broadcasted_iota(jnp.int32, (128, 128), 1)
    alike = (upper >= both) & (upper < 2 * both) & (lower >= both) & (lower < 2 * both)
    alike = alike & (upper // rows == lower // rows)
    ones = jnp.where(alike, 1.0, 0.0).astype(jnp.bfloat16)
    ahead = jnp.where(alike & (upper < lower), 1.0, 0.0).astype(jnp.bfloat16)
    packed = flags.astype(jnp.bfloat16)
    within = jnp.dot(packed, ahead, preferred_element_type=jnp.float32)
    counts = jnp.dot(packed, ones, preferred_element_type=jnp.float32).astype(jnp.bfloat16)
    earlier = lax.broadcasted_iota(jnp.int32, (ranks, ranks), 1) < lax.broadcasted_iota(
        jnp.int32, (ranks, ranks), 0
    )
    before = jnp.dot(
        jnp.where(earlier, 1.0, 0.0).astype(jnp.bfloat16), counts, preferred_element_type=jnp.float32
    )
    slot_of[...] = jnp.where(flags > 0.5, within + before, -1.0).reshape(ranks, 1, 128)

    lane = lax.broadcasted_iota(jnp.int32, (rows, 128), 1)
    row = lax.broadcasted_iota(jnp.int32, (rows, 128), 0)
    slot = lax.broadcasted_iota(jnp.int32, (8 * rows, slots), 1).astype(jnp.float32)

    def core_copy(i, b):
        return pltpu.make_async_remote_copy(
            src_ref=core_out.at[i, b], dst_ref=core_in.at[i, b],
            send_sem=core_send.at[i, b], recv_sem=core_recv.at[i, b],
            device_id={"ep": sibling}, device_id_type=MESH,
        )

    def x_copy(i, b):
        return pltpu.make_async_remote_copy(
            src_ref=x_out.at[i, b], dst_ref=x_in.at[i, b],
            send_sem=x_send.at[i, b], recv_sem=x_recv.at[i, b],
            device_id={"ep": beside}, device_id_type=MESH,
        )

    def z_copy(i, b):
        return pltpu.make_async_remote_copy(
            src_ref=z_out.at[i, b], dst_ref=z_in.at[i, b],
            send_sem=z_send.at[i, b], recv_sem=z_recv.at[i, b],
            device_id={"ep": far if i == 1 else near}, device_id_type=MESH,
        )

    def spread(parts, b):
        factor, place = [], []
        for i in parts:
            plane = 2 * lax.rem(high + 1 - i // 2, 2) + lax.rem(low + 1 - i % 2, 2)
            for other_core in (1, 0):
                for other_x in (1, 0):
                    c = lax.rem(core + other_core, 2)
                    at_x = lax.rem(x + other_x, 2)
                    owner = plane * 4 + at_x * 2 + c
                    note, spot = note_in[owner], slot_of[owner]
                    factor.append(
                        jnp.sum(jnp.where(lane == row + b * rows, note, 0.0), axis=1, keepdims=True)
                    )
                    place.append(
                        jnp.sum(
                            jnp.where(lane == row + (both + b * rows), spot, 0.0),
                            axis=1, keepdims=True,
                        )
                    )
        scale = jnp.concatenate(factor, axis=0)
        pick = jnp.where(jnp.concatenate(place, axis=0) == slot, 1.0, 0.0).astype(jnp.bfloat16)
        for j in range(tiles):
            cut = slice(j * TILE, (j + 1) * TILE)
            part = scale * jnp.dot(pick, produced[b, :, cut], preferred_element_type=jnp.float32)
            for step, i in enumerate(parts):
                top = 4 * rows * step
                core_out[i, b, :, cut] = part[top : top + 2 * rows].astype(jnp.bfloat16)
                core_kept[i, b, :, cut] = part[top + 2 * rows : top + 4 * rows]
        for i in parts:
            core_copy(i, b).start()

    def near_copy(k):
        return pltpu.make_async_remote_copy(
            src_ref=near_out.at[k], dst_ref=near_in.at[k],
            send_sem=near_send.at[k], recv_sem=near_recv.at[k],
            device_id={"ep": near}, device_id_type=MESH,
        )

    def over_cores(i, b):
        core_copy(i, b).wait_recv()
        total = core_kept[i, b] + core_in[i, b].astype(jnp.float32)
        if b == 0:
            x_out[i, b] = total[:rows].astype(jnp.bfloat16)
            x_kept[i, b] = total[rows:]
            x_copy(i, b).start()
        elif i % 2 == 0:
            near_out[i // 2] = total.astype(jnp.bfloat16)
            near_copy(i // 2).start()
        else:
            near_kept[i // 2] = total

    def over_near(i):
        near_copy(i // 2).wait_recv()
        total = near_kept[i // 2] + near_in[i // 2].astype(jnp.float32)
        x_out[i, 1] = total[:rows].astype(jnp.bfloat16)
        x_kept[i, 1] = total[rows:]
        x_copy(i, 1).start()

    def over_x(i, b):
        x_copy(i, b).wait_recv()
        total = x_kept[i, b] + x_in[i, b].astype(jnp.float32)
        if i == 1 and b == 0:
            z_copy(0, b).wait_recv()
            total = total + z_in[0, b].astype(jnp.float32)
        if i < 3:
            z_out[i, b] = total.astype(jnp.bfloat16)
            z_copy(i, b).start()
        else:
            total = total + residual[b].astype(jnp.float32)
            if b == 0:
                z_copy(2, b).wait_recv()
                total = total + z_in[2, b].astype(jnp.float32)
            z_copy(1, b).wait_recv()
            mixed_ref[b] = (total + z_in[1, b].astype(jnp.float32)).astype(jnp.bfloat16)

    spread((0, 1), 1)
    spread((0, 1), 0)
    over_cores(0, 1)
    over_cores(0, 0)
    over_cores(1, 0)
    spread((2, 3), 1)
    over_cores(1, 1)
    spread((2, 3), 0)
    over_cores(2, 1)
    over_x(0, 0)
    over_cores(2, 0)
    over_cores(3, 0)
    over_cores(3, 1)
    over_near(1)

    def note_left(step, carry):
        note_to(lax.rem(me + step, ranks)).wait_send()
        return carry

    over_x(1, 0)
    lax.fori_loop(1, ranks, note_left, 0)
    over_x(2, 0)
    for i in range(4):
        for b in range(batches):
            core_copy(i, b).wait_send()
    over_x(1, 1)
    over_near(3)
    residual_load.wait()
    for i in range(4):
        x_copy(i, 0).wait_send()
    for k in range(2):
        near_copy(k).wait_send()
    over_x(3, 0)
    z_copy(0, 0).wait_send()
    z_copy(2, 0).wait_send()
    x_copy(1, 1).wait_send()
    over_x(3, 1)
    x_copy(3, 1).wait_send()
    z_copy(1, 0).wait_send()
    z_copy(1, 1).wait_send()


def dense_shards(ranks, hidden, down_weight, routes, route_weight, residual):
    batches, rows, chosen = routes.shape
    slots, depth = hidden.shape[2:]
    width = down_weight.shape[2]
    both = batches * rows
    bf16, f32 = jnp.bfloat16, jnp.float32
    sizes = (ranks, batches, rows, chosen, slots, width)
    parts = 4
    return pl.pallas_call(
        functools.partial(dense_kernel, sizes),
        out_shape=jax.ShapeDtypeStruct((batches, rows, width), bf16),
        in_specs=[pl.BlockSpec(memory_space=pl.ANY)] * 5,
        out_specs=pl.BlockSpec(memory_space=pltpu.VMEM),
        scratch_shapes=[
            pltpu.VMEM((batches, slots, depth), bf16),
            pltpu.VMEM((width // TILE, depth, TILE), bf16),
            pltpu.VMEM((batches, chosen, rows), jnp.int32),
            pltpu.VMEM((batches, chosen, rows), f32),
            pltpu.VMEM((batches, rows, width), bf16),
            pltpu.VMEM((batches, slots, width), bf16),
            pltpu.VMEM((ranks, 1, 128), f32),
            pltpu.VMEM((ranks, 1, 128), f32),
            pltpu.VMEM((ranks, 1, 128), f32),
            pltpu.VMEM((parts, batches, 2 * rows, width), bf16),
            pltpu.VMEM((parts, batches, 2 * rows, width), bf16),
            pltpu.VMEM((parts, batches, 2 * rows, width), f32),
            pltpu.VMEM((parts, batches, rows, width), bf16),
            pltpu.VMEM((parts, batches, rows, width), bf16),
            pltpu.VMEM((parts, batches, rows, width), f32),
            pltpu.VMEM((3, batches, rows, width), bf16),
            pltpu.VMEM((3, batches, rows, width), bf16),
            pltpu.VMEM((2, 2 * rows, width), bf16),
            pltpu.VMEM((2, 2 * rows, width), bf16),
            pltpu.VMEM((2, 2 * rows, width), f32),
            pltpu.SemaphoreType.DMA((4,)),
            pltpu.SemaphoreType.DMA((width // TILE,)),
            pltpu.SemaphoreType.DMA((ranks,)),
            pltpu.SemaphoreType.DMA((ranks,)),
            pltpu.SemaphoreType.DMA((parts, batches)),
            pltpu.SemaphoreType.DMA((parts, batches)),
            pltpu.SemaphoreType.DMA((parts, batches)),
            pltpu.SemaphoreType.DMA((parts, batches)),
            pltpu.SemaphoreType.DMA((3, batches)),
            pltpu.SemaphoreType.DMA((3, batches)),
            pltpu.SemaphoreType.DMA((2,)),
            pltpu.SemaphoreType.DMA((2,)),
        ],
        compiler_params=pltpu.CompilerParams(
            collective_id=0, has_side_effects=True, vmem_limit_bytes=48 * 1024 * 1024
        ),
    )(
        *[
            pltpu.with_memory_space_constraint(operand, pltpu.HBM)
            for operand in (
                hidden.reshape(batches, slots, depth),
                down_weight.reshape(depth, width),
                jnp.swapaxes(routes, 1, 2),
                jnp.swapaxes(route_weight, 1, 2),
                residual,
            )
        ]
    )


def solution(mesh):
    ranks = mesh.shape["ep"]
    in_specs = (
        P("dp", "ep", None, None),
        P("ep", None, None),
        P("dp", "ep", None),
        P("dp", "ep", None),
        P("dp", "ep", None),
    )
    out_specs = P("dp", "ep", None)

    def run(hidden, down_weight, routes, route_weight, residual):
        rows = routes.shape[1] // ranks
        batches = routes.shape[0] // mesh.shape["dp"]
        dense = ranks == 16 and rows % 16 == 0 and routes.shape[1] <= hidden.shape[2]
        dense = dense and batches == 2 and 2 * batches * rows <= 128
        body = functools.partial(dense_shards, ranks) if dense else shards
        return jax.shard_map(
            body, mesh=mesh, in_specs=in_specs, out_specs=out_specs, check_vma=False
        )(hidden, down_weight, routes, route_weight, residual)

    return run
```

```python
import functools
import math

import jax
import jax.numpy as jnp
from jax import lax
from jax.experimental import pallas as pl
from jax.experimental.pallas import tpu as pltpu
from jax.sharding import PartitionSpec as P


def shards(hidden, down_weight, routes, route_weight, residual):
    ranks_total = lax.axis_size("ep")
    batch_count = routes.shape[0]
    row_count = routes.shape[1]
    choose_count = routes.shape[2]
    slot_count = hidden.shape[2]
    per_peer = slot_count // ranks_total
    model_width = down_weight.shape[2]
    matrix = down_weight[0]
    labels = jnp.arange(ranks_total, dtype=jnp.int32)
    picked = jnp.sum((routes[:, :, :, None] == labels).astype(jnp.int32), axis=2, dtype=jnp.int32)
    rank_in_block = jnp.take_along_axis(
        jnp.cumsum(picked, axis=1, dtype=jnp.int32) - picked, routes, axis=2
    )
    loads_out = jnp.transpose(jnp.sum(picked, axis=1, dtype=jnp.int32))
    loads_in = lax.all_to_all(loads_out, "ep", split_axis=0, concat_axis=0, tiled=True)
    arriving = jnp.transpose(loads_in)
    offsets = jnp.cumsum(arriving, axis=1, dtype=jnp.int32) - arriving
    totals = jnp.sum(arriving, axis=1, dtype=jnp.int32)
    results = []
    for batch_index in range(batch_count):
        packed = hidden[batch_index, 0]
        block_size = math.gcd(slot_count, 128)

        def add_block(block_index, produced_in):
            begin_at = block_index * block_size
            segment = lax.dynamic_slice_in_dim(packed, begin_at, block_size, 0)
            product = jnp.dot(segment, matrix, preferred_element_type=jnp.float32).astype(
                jnp.bfloat16
            )
            return lax.dynamic_update_slice_in_dim(produced_in, product, begin_at, 0)

        block_count = (totals[batch_index] + block_size - 1) // block_size
        expert_produced = lax.fori_loop(
            0, block_count, add_block, jnp.zeros((slot_count, model_width), jnp.bfloat16)
        )
        selector = offsets[batch_index][:, None] + jnp.arange(per_peer, dtype=jnp.int32)[None, :]
        selector = jnp.minimum(selector, slot_count - 1)
        sending = jnp.take(expert_produced, selector.reshape(-1), axis=0).reshape(
            ranks_total, per_peer, model_width
        )
        arrived = lax.all_to_all(sending, "ep", split_axis=0, concat_axis=0, tiled=True)
        flattened = arrived.reshape(ranks_total * per_peer, model_width)
        location = routes[batch_index] * per_peer + rank_in_block[batch_index]
        gathered = jnp.take(flattened, location.reshape(-1), axis=0).reshape(
            row_count, choose_count, model_width
        )
        weighted = jnp.sum(
            route_weight[batch_index][:, :, None] * gathered.astype(jnp.float32), axis=1
        )
        results.append((residual[batch_index].astype(jnp.float32) + weighted).astype(jnp.bfloat16))
    return jnp.stack(results, axis=0)


MESH = pl.DeviceIdType.MESH
TILE = 512


def dense_kernel(
    sizes, hidden_hbm, weight_hbm, routes_hbm, shares_hbm, residual_hbm, mixed_ref,
    hidden, weight, routes, shares, residual, produced,
    note_out, note_in, slot_of,
    core_out, core_in, core_kept, x_out, x_in, x_kept, z_out, z_in, near_out, near_in, near_kept,
    load_sem, column_sem, note_send, note_recv, core_send, core_recv, x_send, x_recv, z_send, z_recv,
    near_send, near_recv,
):
    ranks, batches, rows, chosen, slots, width = sizes
    both = batches * rows
    me = lax.axis_index("ep")
    core, x, z = lax.rem(me, 2), lax.rem(me // 2, 2), me // 4
    low, high = lax.rem(z, 2), z // 2
    sibling = me + 1 - 2 * core
    beside = me + 2 - 4 * x
    near = me + 4 - 8 * low
    far = me + 8 - 16 * high

    barrier = pltpu.get_barrier_semaphore()

    turn = 2 * (me // (ranks // 2)) - 1

    def peer_of(step):
        return lax.rem(2 * ranks - 1 - me + turn * step, ranks)

    def greet(step, carry):
        peer = peer_of(step)

        @pl.when(peer != me)
        def _():
            pl.semaphore_signal(barrier, inc=1, device_id={"ep": peer}, device_id_type=MESH)

        return carry

    loads = [
        pltpu.make_async_copy(routes_hbm, routes, load_sem.at[0]),
        pltpu.make_async_copy(shares_hbm, shares, load_sem.at[1]),
        pltpu.make_async_copy(hidden_hbm, hidden, load_sem.at[2]),
    ]
    columns = [
        pltpu.make_async_copy(
            weight_hbm.at[:, pl.ds(j * TILE, TILE)], weight.at[j], column_sem.at[j]
        )
        for j in range(width // TILE)
    ]
    residual_load = pltpu.make_async_copy(residual_hbm, residual, load_sem.at[3])
    loads[0].start()
    loads[1].start()
    lax.fori_loop(0, ranks, greet, 0)
    for copy in loads[2:] + columns + [residual_load]:
        copy.start()

    loads[0].wait()
    loads[1].wait()
    given, named = [], []
    expert = lax.broadcasted_iota(jnp.int32, (ranks, chosen, rows), 0)
    for b in range(batches):
        hit = routes[b][None] == expert
        given.append(jnp.sum(jnp.where(hit, shares[b][None], 0.0), axis=1))
        named.append(jnp.sum(jnp.where(hit, 1.0, 0.0), axis=1))
    notes = jnp.concatenate(
        given + named + [jnp.zeros((ranks, 128 - 2 * both), jnp.float32)], axis=1
    )
    note_out[...] = notes.reshape(ranks, 1, 128)
    note_in[pl.ds(me, 1)] = note_out[pl.ds(me, 1)]

    pl.semaphore_wait(barrier, ranks - 1)

    def note_to(peer):
        return pltpu.make_async_remote_copy(
            src_ref=note_out.at[peer],
            dst_ref=note_in.at[me],
            send_sem=note_send.at[peer],
            recv_sem=note_recv.at[me],
            device_id={"ep": peer},
            device_id_type=MESH,
        )

    def note_from(step):
        peer = lax.rem(me + step, ranks)
        return pltpu.make_async_remote_copy(
            src_ref=note_out.at[peer],
            dst_ref=note_in.at[peer],
            send_sem=note_send.at[peer],
            recv_sem=note_recv.at[peer],
            device_id={"ep": peer},
            device_id_type=MESH,
        )

    def send_note(step, carry):
        peer = peer_of(step)

        @pl.when(peer != me)
        def _():
            note_to(peer).start()

        return carry

    lax.fori_loop(0, ranks, send_note, 0)

    def produce(b, tiles):
        for j in tiles:
            if b == 0:
                columns[j].wait()
            produced[b, :, j * TILE : (j + 1) * TILE] = jnp.dot(
                hidden[b], weight[j], preferred_element_type=jnp.float32
            ).astype(jnp.bfloat16)

    tiles = width // TILE
    loads[2].wait()
    produce(0, range(tiles))
    produce(1, range(tiles))

    def take_note(step, carry):
        note_from(step).wait_recv()
        return carry

    lax.fori_loop(1, ranks, take_note, 0)

    flags = note_in[...].reshape(ranks, 128)
    upper = lax.broadcasted_iota(jnp.int32, (128, 128), 0)
    lower = lax.broadcasted_iota(jnp.int32, (128, 128), 1)
    alike = (upper >= both) & (upper < 2 * both) & (lower >= both) & (lower < 2 * both)
    alike = alike & (upper // rows == lower // rows)
    ones = jnp.where(alike, 1.0, 0.0).astype(jnp.bfloat16)
    ahead = jnp.where(alike & (upper < lower), 1.0, 0.0).astype(jnp.bfloat16)
    packed = flags.astype(jnp.bfloat16)
    within = jnp.dot(packed, ahead, preferred_element_type=jnp.float32)
    counts = jnp.dot(packed, ones, preferred_element_type=jnp.float32).astype(jnp.bfloat16)
    earlier = lax.broadcasted_iota(jnp.int32, (ranks, ranks), 1) < lax.broadcasted_iota(
        jnp.int32, (ranks, ranks), 0
    )
    before = jnp.dot(
        jnp.where(earlier, 1.0, 0.0).astype(jnp.bfloat16), counts, preferred_element_type=jnp.float32
    )
    slot_of[...] = jnp.where(flags > 0.5, within + before, -1.0).reshape(ranks, 1, 128)

    lane = lax.broadcasted_iota(jnp.int32, (rows, 128), 1)
    row = lax.broadcasted_iota(jnp.int32, (rows, 128), 0)
    slot = lax.broadcasted_iota(jnp.int32, (8 * rows, slots), 1).astype(jnp.float32)

    def core_copy(i, b):
        return pltpu.make_async_remote_copy(
            src_ref=core_out.at[i, b], dst_ref=core_in.at[i, b],
            send_sem=core_send.at[i, b], recv_sem=core_recv.at[i, b],
            device_id={"ep": sibling}, device_id_type=MESH,
        )

    def x_copy(i, b):
        return pltpu.make_async_remote_copy(
            src_ref=x_out.at[i, b], dst_ref=x_in.at[i, b],
            send_sem=x_send.at[i, b], recv_sem=x_recv.at[i, b],
            device_id={"ep": beside}, device_id_type=MESH,
        )

    def z_copy(i, b):
        return pltpu.make_async_remote_copy(
            src_ref=z_out.at[i, b], dst_ref=z_in.at[i, b],
            send_sem=z_send.at[i, b], recv_sem=z_recv.at[i, b],
            device_id={"ep": far if i == 1 else near}, device_id_type=MESH,
        )

    def spread(parts, b):
        factor, place = [], []
        for i in parts:
            plane = 2 * lax.rem(high + 1 - i // 2, 2) + lax.rem(low + 1 - i % 2, 2)
            for other_core in (1, 0):
                for other_x in (1, 0):
                    c = lax.rem(core + other_core, 2)
                    at_x = lax.rem(x + other_x, 2)
                    owner = plane * 4 + at_x * 2 + c
                    note, spot = note_in[owner], slot_of[owner]
                    factor.append(
                        jnp.sum(jnp.where(lane == row + b * rows, note, 0.0), axis=1, keepdims=True)
                    )
                    place.append(
                        jnp.sum(
                            jnp.where(lane == row + (both + b * rows), spot, 0.0),
                            axis=1, keepdims=True,
                        )
                    )
        scale = jnp.concatenate(factor, axis=0)
        pick = jnp.where(jnp.concatenate(place, axis=0) == slot, 1.0, 0.0).astype(jnp.bfloat16)
        for j in range(tiles):
            cut = slice(j * TILE, (j + 1) * TILE)
            part = scale * jnp.dot(pick, produced[b, :, cut], preferred_element_type=jnp.float32)
            for step, i in enumerate(parts):
                top = 4 * rows * step
                core_out[i, b, :, cut] = part[top : top + 2 * rows].astype(jnp.bfloat16)
                core_kept[i, b, :, cut] = part[top + 2 * rows : top + 4 * rows]
        for i in parts:
            core_copy(i, b).start()

    def near_copy(k):
        return pltpu.make_async_remote_copy(
            src_ref=near_out.at[k], dst_ref=near_in.at[k],
            send_sem=near_send.at[k], recv_sem=near_recv.at[k],
            device_id={"ep": near}, device_id_type=MESH,
        )

    def over_cores(i, b):
        core_copy(i, b).wait_recv()
        total = core_kept[i, b] + core_in[i, b].astype(jnp.float32)
        if b == 0:
            x_out[i, b] = total[:rows].astype(jnp.bfloat16)
            x_kept[i, b] = total[rows:]
            x_copy(i, b).start()
        elif i % 2 == 0:
            near_out[i // 2] = total.astype(jnp.bfloat16)
            near_copy(i // 2).start()
        else:
            near_kept[i // 2] = total

    def over_near(i):
        near_copy(i // 2).wait_recv()
        total = near_kept[i // 2] + near_in[i // 2].astype(jnp.float32)
        x_out[i, 1] = total[:rows].astype(jnp.bfloat16)
        x_kept[i, 1] = total[rows:]
        x_copy(i, 1).start()

    def over_x(i, b):
        x_copy(i, b).wait_recv()
        total = x_kept[i, b] + x_in[i, b].astype(jnp.float32)
        if i == 1 and b == 0:
            z_copy(0, b).wait_recv()
            total = total + z_in[0, b].astype(jnp.float32)
        if i < 3:
            z_out[i, b] = total.astype(jnp.bfloat16)
            z_copy(i, b).start()
        else:
            total = total + residual[b].astype(jnp.float32)
            if b == 0:
                z_copy(2, b).wait_recv()
                total = total + z_in[2, b].astype(jnp.float32)
            z_copy(1, b).wait_recv()
            mixed_ref[b] = (total + z_in[1, b].astype(jnp.float32)).astype(jnp.bfloat16)

    spread((0, 1), 0)
    spread((0, 1), 1)
    over_cores(0, 0)
    over_cores(1, 0)
    over_cores(0, 1)
    over_cores(1, 1)
    spread((2, 3), 0)
    over_cores(2, 0)
    over_x(0, 0)
    over_cores(3, 0)
    spread((2, 3), 1)
    over_near(1)
    over_cores(2, 1)
    over_cores(3, 1)
    def note_left(step, carry):
        note_to(lax.rem(me + step, ranks)).wait_send()
        return carry

    over_x(1, 0)
    lax.fori_loop(1, ranks, note_left, 0)
    over_x(2, 0)
    for i in range(4):
        for b in range(batches):
            core_copy(i, b).wait_send()
    over_x(1, 1)
    over_near(3)
    residual_load.wait()
    for i in range(4):
        x_copy(i, 0).wait_send()
    for k in range(2):
        near_copy(k).wait_send()
    over_x(3, 0)
    z_copy(0, 0).wait_send()
    z_copy(2, 0).wait_send()
    x_copy(1, 1).wait_send()
    over_x(3, 1)
    x_copy(3, 1).wait_send()
    z_copy(1, 0).wait_send()
    z_copy(1, 1).wait_send()


def dense_shards(ranks, hidden, down_weight, routes, route_weight, residual):
    batches, rows, chosen = routes.shape
    slots, depth = hidden.shape[2:]
    width = down_weight.shape[2]
    both = batches * rows
    bf16, f32 = jnp.bfloat16, jnp.float32
    sizes = (ranks, batches, rows, chosen, slots, width)
    parts = 4
    return pl.pallas_call(
        functools.partial(dense_kernel, sizes),
        out_shape=jax.ShapeDtypeStruct((batches, rows, width), bf16),
        in_specs=[pl.BlockSpec(memory_space=pl.ANY)] * 5,
        out_specs=pl.BlockSpec(memory_space=pltpu.VMEM),
        scratch_shapes=[
            pltpu.VMEM((batches, slots, depth), bf16),
            pltpu.VMEM((width // TILE, depth, TILE), bf16),
            pltpu.VMEM((batches, chosen, rows), jnp.int32),
            pltpu.VMEM((batches, chosen, rows), f32),
            pltpu.VMEM((batches, rows, width), bf16),
            pltpu.VMEM((batches, slots, width), bf16),
            pltpu.VMEM((ranks, 1, 128), f32),
            pltpu.VMEM((ranks, 1, 128), f32),
            pltpu.VMEM((ranks, 1, 128), f32),
            pltpu.VMEM((parts, batches, 2 * rows, width), bf16),
            pltpu.VMEM((parts, batches, 2 * rows, width), bf16),
            pltpu.VMEM((parts, batches, 2 * rows, width), f32),
            pltpu.VMEM((parts, batches, rows, width), bf16),
            pltpu.VMEM((parts, batches, rows, width), bf16),
            pltpu.VMEM((parts, batches, rows, width), f32),
            pltpu.VMEM((3, batches, rows, width), bf16),
            pltpu.VMEM((3, batches, rows, width), bf16),
            pltpu.VMEM((2, 2 * rows, width), bf16),
            pltpu.VMEM((2, 2 * rows, width), bf16),
            pltpu.VMEM((2, 2 * rows, width), f32),
            pltpu.SemaphoreType.DMA((4,)),
            pltpu.SemaphoreType.DMA((width // TILE,)),
            pltpu.SemaphoreType.DMA((ranks,)),
            pltpu.SemaphoreType.DMA((ranks,)),
            pltpu.SemaphoreType.DMA((parts, batches)),
            pltpu.SemaphoreType.DMA((parts, batches)),
            pltpu.SemaphoreType.DMA((parts, batches)),
            pltpu.SemaphoreType.DMA((parts, batches)),
            pltpu.SemaphoreType.DMA((3, batches)),
            pltpu.SemaphoreType.DMA((3, batches)),
            pltpu.SemaphoreType.DMA((2,)),
            pltpu.SemaphoreType.DMA((2,)),
        ],
        compiler_params=pltpu.CompilerParams(
            collective_id=0, has_side_effects=True, vmem_limit_bytes=48 * 1024 * 1024
        ),
    )(
        *[
            pltpu.with_memory_space_constraint(operand, pltpu.HBM)
            for operand in (
                hidden.reshape(batches, slots, depth),
                down_weight.reshape(depth, width),
                jnp.swapaxes(routes, 1, 2),
                jnp.swapaxes(route_weight, 1, 2),
                residual,
            )
        ]
    )


def solution(mesh):
    ranks = mesh.shape["ep"]
    in_specs = (
        P("dp", "ep", None, None),
        P("ep", None, None),
        P("dp", "ep", None),
        P("dp", "ep", None),
        P("dp", "ep", None),
    )
    out_specs = P("dp", "ep", None)

    def run(hidden, down_weight, routes, route_weight, residual):
        rows = routes.shape[1] // ranks
        batches = routes.shape[0] // mesh.shape["dp"]
        dense = ranks == 16 and rows % 16 == 0 and routes.shape[1] <= hidden.shape[2]
        dense = dense and batches == 2 and 2 * batches * rows <= 128
        body = functools.partial(dense_shards, ranks) if dense else shards
        return jax.shard_map(
            body, mesh=mesh, in_specs=in_specs, out_specs=out_specs, check_vma=False
        )(hidden, down_weight, routes, route_weight, residual)

    return run
```
